128 devices in a mesh: dp: 8 (over y, core), space: 16 (over x, z).
Axes of the slice: x: 4, y: 4, z: 4, core: 2. Of those that a mesh axis runs over, the one named last changes fastest.
Arguments:
- activations: bfloat16 [2, 8, 8, 32, 32, 768], P(None, 'dp', None, 'space'), may hold values from -60 to 60
- out_grads: bfloat16 [2, 8, 8, 32, 32, 768], P(None, 'dp', None, 'space'), may hold values from -6 to 6
- omega: bfloat16 [768, 128], replicated, may hold values from -0.21875 to 0.21875
Outputs:
- basis: float32 [2, 20736, 128], P(None, ('dp', 'space'))
The draws below stay inside these ranges and needn't reach their ends.
All inputs are finite; a program needn't handle non-finite values.
Results may differ from the reference program's by a relative error of at most 0.0033.
Values may be sent and summed in bfloat16 or wider, within the bound.
A program may use at most 128 MiB of HBM per device.

```python
import math
import jax
import jax.numpy as jnp
from jax import lax

C = 768
RANK = 128
LAYERS = 2
FRAMES = 8
WCOLS = 32
BATCH = 8
HEIGHT = 32
KROWS = 20736


def draw_activations(key, part):
    scale_key, base_key = jax.random.split(key, 2)
    shape = (LAYERS, BATCH, FRAMES, HEIGHT, WCOLS, C)
    scales = jnp.exp(jax.random.uniform(scale_key, (LAYERS, 1, 1, 1, 1, C), jnp.float32, 0.0, math.log(10.0)))
    base = jnp.clip(jax.random.normal(base_key, shape, jnp.float32), -6.0, 6.0)
    return (base * scales).astype(jnp.bfloat16)


def steps_of(own_key, shape, shards, smallest, largest):
    loudness = 1.0
    for axis_at, parts in shards:
        draws = jax.random.uniform(jax.random.fold_in(jax.random.fold_in(own_key, 6), axis_at), (parts,), jnp.float32, smallest / len(shards), largest / len(shards))
        loudness = loudness * jnp.repeat(jnp.exp(draws), shape[axis_at] // parts).reshape((-1,) + (1,) * (len(shape) - 1 - axis_at))
    return loudness


def normal_values(key, dims, scale, reach, shards=(), held_as=jnp.bfloat16):
    values = jax.random.normal(key, dims, jnp.float32) * scale
    if len(shards) > 0:
        values = steps_of(key, dims, shards, -0.22, 0.18) * values
    return jnp.clip(values, min=-reach, max=reach).astype(held_as)


def setup_inputs(seed: int = 0) -> dict:
    key_of = jax.random.split(jax.random.key(seed), 4)
    return {
        "activations": draw_activations(jax.random.fold_in(key_of[3], 71), 0),
        "out_grads": normal_values(key_of[1], (LAYERS, BATCH, FRAMES, HEIGHT, WCOLS, C), 1.0, 6.0, ((1, 8), (3, 16))),
        "omega": normal_values(key_of[2], (C, RANK), C ** -0.5, 0.21875),
    }


def reference(activations, out_grads, omega):
    results = []
    for layer in range(LAYERS):
        grads_flat = out_grads[layer].reshape(-1, C)
        sketched = jnp.dot(grads_flat.astype(jnp.float32), omega.astype(jnp.float32), preferred_element_type=jnp.float32).astype(jnp.bfloat16)
        padded = jnp.pad(activations[layer], ((0, 0), (1, 1), (1, 1), (1, 1), (0, 0)))
        blocks = []
        for along_t in range(3):
            for along_h in range(3):
                for along_w in range(3):
                    window = padded[:, along_t:along_t + FRAMES, along_h:along_h + HEIGHT, along_w:along_w + WCOLS, :]
                    window = window.reshape(-1, C)
                    blocks.append(jnp.dot(window.T.astype(jnp.float32), sketched.astype(jnp.float32), preferred_element_type=jnp.float32))
        sketch = jnp.concatenate(blocks, axis=0)
        gram = jnp.dot(sketch.T, sketch, precision=lax.Precision.HIGHEST)
        lower = jnp.linalg.cholesky(gram)
        basis = jax.scipy.linalg.solve_triangular(lower, sketch.T, lower=True).T
        results.append(basis * math.sqrt(KROWS))
    return jnp.stack(results)
```

```python
import functools
import math

import jax
import jax.numpy as jnp
from jax import lax
from jax.experimental import pallas as pl
from jax.experimental.pallas import tpu as pltpu
from jax.sharding import PartitionSpec as P

MESH = pl.DeviceIdType.MESH
BF16, F32 = jnp.bfloat16, jnp.float32
HIGHEST = lax.Precision.HIGHEST
RING = 4
OWN = 162
WIN = 176
BLOCK = OWN * 16
SLAB = 6
ORDER = (2, 1, 3, 0)
CHUNKS = [(r, l) for r in ORDER for l in (0, 1)]
PANEL = 8
STAGE2 = BF16


def reduce_kernel(
    act, grads, omega, rows_out, gram_out,
    act2, act_t, sk, ext, slab, send1, recv1, send2, recv2, part1,
    send3, recv3, send4, recv4, part2, recv5,
    gram, half, recv6, recv7, ssem, rsem,
):
    layers, _, frames, height, width, channels = act.shape
    rank = omega.shape[1]
    dp, space = lax.axis_index("dp"), lax.axis_index("space")
    y, core = dp // 2, dp % 2
    x, z = space // RING, space % RING
    other_dp = y * 2 + 1 - core

    def along(axis, step):
        if axis == "x":
            return {"dp": dp, "space": (x + step) % RING * RING + z}
        if axis == "z":
            return {"dp": dp, "space": x * RING + (z + step) % RING}
        return {"dp": (y + step) % RING * 2 + core, "space": space}

    partner = {"dp": other_dp, "space": space}
    spaces = RING * RING
    below, above = (space + 1) % spaces, (space + spaces - 1) % spaces
    halo = [
        {"dp": to, "space": at} for at in (below, above) for to in (dp, other_dp)
    ]
    peers = [partner] + halo + [along(a, j) for a in ("x", "y", "z") for j in (1, 2, 3)]

    barrier = pltpu.get_barrier_semaphore()
    for peer in peers:
        pl.semaphore_signal(barrier, inc=1, device_id=peer, device_id_type=MESH)
    pl.semaphore_wait(barrier, len(peers))

    sent = []

    def send(src, dst, to):
        at = len(sent)
        copy = pltpu.make_async_remote_copy(
            src_ref=src, dst_ref=dst, send_sem=ssem.at[at], recv_sem=rsem.at[at],
            device_id=to, device_id_type=MESH,
        )
        copy.start()
        sent.append(copy)
        return copy

    act_copies, sk_copies = [], []
    for l in range(layers):
        for h in range(height):
            flat = grads[l, 0, :, h].reshape(frames * width, channels)
            value = jnp.dot(flat, omega[...], preferred_element_type=F32).astype(BF16)
            sk[l, 0, 1 + h] = value.reshape(frames, width, rank)
        copies = []
        for slot, to in ((0, 0), (1, 1)):
            copies.append(send(sk.at[l, 0, height], sk.at[l, slot, 0], halo[to]))
            copies.append(send(sk.at[l, 0, 1], sk.at[l, slot, height + 1], halo[2 + to]))
        copies.append(send(sk.at[l, 0, 1:1 + height], sk.at[l, 1, 1:1 + height], partner))
        sk_copies.append(copies)
        act_copies.append(send(act.at[l], act2.at[l], partner))

    def transpose(l, slot, source):
        for h in range(height):
            flat = source[l, 0, :, h].reshape(frames * width, channels)
            at = (slot * height + h) * frames * width
            act_t[l, :, at:at + frames * width] = flat.T

    for l in range(layers):
        transpose(l, 0, act)

    column = lax.broadcasted_iota(jnp.int32, (frames * width, rank), 0) % width
    for l in range(layers):
        for copy in sk_copies[l]:
            copy.wait_recv()
        for slot in range(2):
            for h in range(height + 2):
                value = sk[l, slot, h].reshape(frames * width, rank).astype(F32)
                if h == 0:
                    value = jnp.where(space > 0, value, 0.0)
                if h == height + 1:
                    value = jnp.where(space < spaces - 1, value, 0.0)
                ahead = jnp.where(column < width - 1, pltpu.roll(value, frames * width - 1, 0), 0.0)
                behind = jnp.where(column > 0, pltpu.roll(value, 1, 0), 0.0)
                for c, shifted in enumerate((ahead, value, behind)):
                    zero = jnp.zeros((width, rank), BF16)
                    ext[l, c, slot, h, 0] = zero
                    ext[l, c, slot, h, frames + 1] = zero
                    ext[l, c, slot, h, 1:1 + frames] = shifted.astype(BF16).reshape(frames, width, rank)
        act_copies[l].wait_recv()
        transpose(l, 1, act2)

    depth = 2 * height * frames * width

    def compute(n, r, l):
        owner = (y + r) % RING * 2 + core
        first = 27 * owner // 8

        def columns(k):
            k = jnp.minimum(first + k, 26)
            a, b, c = k // 9, k // 3 % 3, k % 3
            return ext[l, c, :, pl.ds(2 - b, height), pl.ds(2 - a, frames)].reshape(depth, rank)

        def pair(i, _):
            both = jnp.concatenate([columns(2 * i), columns(2 * i + 1)], axis=1)
            for m in range(3):
                rows = channels // 3
                value = jnp.dot(act_t[l, m * rows:(m + 1) * rows], both, preferred_element_type=F32)
                for s in range(2):
                    at = pl.multiple_of((2 * i + s) * channels + m * rows, rows)
                    slab[n, pl.ds(at, rows)] = value[:, s * rank:(s + 1) * rank]
            return 0

        lax.fori_loop(0, SLAB // 2, pair, 0)

    def window(n, r, l, mine, other):
        owner = (y + r) % RING * 2 + core
        place = mine * RING + other if l == 0 else other * RING + mine
        at = 27 * owner % 8 * (channels // 8) + OWN * place // 16 * 16
        return slab[n, pl.ds(pl.multiple_of(at, 16), WIN)]

    first_axis = ("x", "z")
    last_axis = ("z", "x")
    first_at = (x, z)
    last_at = (z, x)
    half1 = RING // 2
    step1, step2, step3, step4, step5 = {}, {}, {}, {}, {}

    def start1(n):
        r, l = CHUNKS[n]
        for o in range(RING):
            send1[n, o] = window(n, r, l, (first_at[l] + 2) % RING, o).astype(BF16)
        step1[n] = [
            send(send1.at[n, :half1], recv1.at[n, :half1], along(first_axis[l], 1)),
            send(send1.at[n, half1:], recv1.at[n, half1:], along(first_axis[l], 3)),
        ]

    def start2(n):
        r, l = CHUNKS[n]
        copies = []
        for s, step in enumerate((1, 3)):
            step1[n][s].wait_recv()
            for o in range(RING):
                value = window(n, r, l, (first_at[l] + step) % RING, o)
                if (o < half1) == (s == 0):
                    value = value + recv1[n, o].astype(F32)
                send2[n, s, o] = value.astype(BF16)
            copies.append(send(send2.at[n, s], recv2.at[n, s], along(first_axis[l], step)))
        step2[n] = copies

    def finish1(n):
        r, l = CHUNKS[n]
        for copy in step2[n]:
            copy.wait_recv()
        if r in (1, 3):
            step3[l][0 if r == 1 else 1].wait_recv()
        if r == 0:
            for copy in step4[l]:
                copy.wait_recv()
        for o in range(RING):
            value = window(n, r, l, first_at[l], o)
            value = value + recv2[n, 0, o].astype(F32) + recv2[n, 1, o].astype(F32)
            if r == 2:
                send3[l, o] = value.astype(STAGE2)
            elif r == 0:
                part2[l, o] = value + recv4[l, 0, o].astype(F32) + recv4[l, 1, o].astype(F32)
            else:
                s = 0 if r == 1 else 1
                if (o < half1) == (s == 0):
                    value = value + recv3[l, o].astype(F32)
                send4[l, s, o] = value.astype(STAGE2)
        if r == 2:
            step3[l] = [
                send(send3.at[l, :half1], recv3.at[l, :half1], along("y", 1)),
                send(send3.at[l, half1:], recv3.at[l, half1:], along("y", 3)),
            ]
        elif r == 0:
            step5[l] = [
                send(part2.at[l, (last_at[l] + j) % RING], recv5.at[l, j - 1], along(last_axis[l], j))
                for j in (1, 2, 3)
            ]
        else:
            s = 0 if r == 1 else 1
            step4.setdefault(l, []).append(send(send4.at[l, s], recv4.at[l, s], along("y", r)))

    total = len(CHUNKS)
    for n in range(total + 3):
        if n < total:
            compute(n, *CHUNKS[n])
            start1(n)
        if 1 <= n <= total:
            start2(n - 1)
        if n >= 3:
            finish1(n - 3)

    shift = 2 * space % 16
    row = lax.broadcasted_iota(jnp.int32, (WIN, rank), 0)
    for l in range(layers):
        for copy in step5[l]:
            copy.wait_recv()
        value = part2[l, last_at[l]] + recv5[l, 0] + recv5[l, 1] + recv5[l, 2]
        value = pltpu.roll(value, (WIN - shift) % WIN, 0)
        value = jnp.where(row < OWN, value, 0.0)
        rows_out[l] = value
        gram[l] = lax.dot_general(
            value, value, (((0,), (0,)), ((), ())), precision=HIGHEST, preferred_element_type=F32
        )

    part = rank // 2
    keep = pl.multiple_of(core * part, part)
    give = pl.multiple_of((1 - core) * part, part)
    copy = send(gram.at[:, pl.ds(give, part)], recv6, partner)
    copy.wait_recv()
    half[0] = gram[:, pl.ds(keep, part)] + recv6[...]
    for s, axis in enumerate(("y", "x", "z")):
        copies = [send(half.at[s], recv7.at[s, j - 1], along(axis, j)) for j in (1, 2, 3)]
        for copy in copies:
            copy.wait_recv()
        half[s + 1] = half[s] + recv7[s, 0] + recv7[s, 1] + recv7[s, 2]
    copy = send(half.at[3], gram_out.at[:, pl.ds(keep, part)], partner)
    gram_out[:, pl.ds(keep, part)] = half[3]
    copy.wait_recv()
    for copy in sent:
        copy.wait_send()


def factor_kernel(rows, gram, out, work, inverse, *, scale):
    layers, rank, _ = gram.shape
    lane = lax.broadcasted_iota(jnp.int32, (PANEL, rank), 1)
    row = lax.broadcasted_iota(jnp.int32, (PANEL, rank), 0)
    wide = lax.broadcasted_iota(jnp.int32, (rank, rank), 1)
    work[...] = gram[...]
    for p in range(rank // PANEL):
        first = p * PANEL
        for l in range(layers):
            panel = work[l, first:first + PANEL]
            cols = [
                jnp.broadcast_to(panel[:, first + j:first + j + 1], (PANEL, rank)) for j in range(PANEL)
            ]
            pivots = jnp.ones((PANEL, rank), F32)
            for j in range(PANEL):
                pivot = jnp.broadcast_to(cols[j][j:j + 1], (PANEL, rank))
                pivots = jnp.where(row == j, pivot, pivots)
                if j < PANEL - 1:
                    mult = jnp.where(row > j, cols[j] / pivot, 0.0)
                    updated = panel - mult * panel[j:j + 1]
                    panel = jnp.where((lane == first + j) & (row > j), -mult, updated)
                    for i in range(j + 1, PANEL):
                        cols[i] = cols[i] - mult * cols[i][j:j + 1]
            inside = (lane >= first) & (lane < first + PANEL)
            unit = jnp.where(lane - first < row, panel, jnp.where(lane - first == row, 1.0, 0.0))
            full = jnp.where(inside, unit, panel)
            inverse[l, first:first + PANEL] = jnp.where(lane - first <= row, full, 0.0) / jnp.sqrt(pivots)
            if first + PANEL < rank:
                step = lax.dot_general(
                    panel / pivots, full, (((0,), (0,)), ((), ())),
                    precision=HIGHEST, preferred_element_type=F32,
                )
                rest = first + PANEL
                in_wide = (wide[rest:] >= first) & (wide[rest:] < rest)
                work[l, rest:] = jnp.where(in_wide, 0.0, work[l, rest:]) - step[rest:]
    for l in range(layers):
        value = lax.dot_general(
            rows[l], inverse[l], (((1,), (1,)), ((), ())),
            precision=HIGHEST, preferred_element_type=F32,
        )
        out[l] = (value * scale)[:OWN]


def shards(activations, out_grads, omega):
    layers, clips, frames, height, width, channels = activations.shape
    rank = omega.shape[1]
    chunks = len(CHUNKS)
    vmem = pl.BlockSpec(memory_space=pltpu.VMEM)
    blocks = (RING, WIN, rank)
    rows, gram = pl.pallas_call(
        reduce_kernel,
        name="reduce",
        out_shape=(
            jax.ShapeDtypeStruct((layers, WIN, rank), F32),
            jax.ShapeDtypeStruct((layers, rank, rank), F32),
        ),
        in_specs=[vmem] * 3,
        out_specs=(vmem, vmem),
        scratch_shapes=[
            pltpu.VMEM(activations.shape, BF16),
            pltpu.VMEM((layers, channels, 2 * height * frames * width), BF16),
            pltpu.VMEM((layers, 2, height + 2, frames, width, rank), BF16),
            pltpu.VMEM((layers, 3, 2, height + 2, frames + 2, width, rank), BF16),
            pltpu.VMEM((chunks, SLAB * channels, rank), F32),
            pltpu.VMEM((chunks,) + blocks, BF16),
            pltpu.VMEM((chunks,) + blocks, BF16),
            pltpu.VMEM((chunks, 2) + blocks, BF16),
            pltpu.VMEM((chunks, 2) + blocks, BF16),
            pltpu.VMEM((8, 128), F32),
            pltpu.VMEM((layers,) + blocks, STAGE2),
            pltpu.VMEM((layers,) + blocks, STAGE2),
            pltpu.VMEM((layers, 2) + blocks, STAGE2),
            pltpu.VMEM((layers, 2) + blocks, STAGE2),
            pltpu.VMEM((layers,) + blocks, F32),
            pltpu.VMEM((layers, 3, WIN, rank), F32),
            pltpu.VMEM((layers, rank, rank), F32),
            pltpu.VMEM((4, layers, rank // 2, rank), F32),
            pltpu.VMEM((layers, rank // 2, rank), F32),
            pltpu.VMEM((3, 3, layers, rank // 2, rank), F32),
            pltpu.SemaphoreType.DMA((80,)),
            pltpu.SemaphoreType.DMA((80,)),
        ],
        compiler_params=pltpu.CompilerParams(
            collective_id=0, has_side_effects=True, vmem_limit_bytes=60 * 2**20
        ),
    )(activations, out_grads, omega)
    return pl.pallas_call(
        functools.partial(factor_kernel, scale=math.sqrt(27 * channels)),
        name="factor",
        out_shape=jax.ShapeDtypeStruct((layers, OWN, rank), F32),
        in_specs=[vmem] * 2,
        out_specs=vmem,
        scratch_shapes=[
            pltpu.VMEM((layers, rank, rank), F32),
            pltpu.VMEM((layers, rank, rank), F32),
        ],
    )(rows, gram)


def solution(mesh):
    return jax.shard_map(
        shards,
        mesh=mesh,
        in_specs=(
            P(None, "dp", None, "space", None, None),
            P(None, "dp", None, "space", None, None),
            P(),
        ),
        out_specs=P(None, ("dp", "space"), None),
        check_vma=False,
    )
```

```python
import functools
import math

import jax
import jax.numpy as jnp
from jax import lax
from jax.experimental import pallas as pl
from jax.experimental.pallas import tpu as pltpu
from jax.sharding import PartitionSpec as P

MESH = pl.DeviceIdType.MESH
BF16, F32 = jnp.bfloat16, jnp.float32
HIGHEST = lax.Precision.HIGHEST
RING = 4
OWN = 162
WIN = 176
BLOCK = OWN * 16
SLAB = 6
ORDER = (2, 1, 3, 0)
CHUNKS = [(r, l) for r in ORDER for l in (0, 1)]
PANEL = 8
LAG2, LAG3 = 2, 4
STAGE2 = BF16


def reduce_kernel(
    act_in, grads_in, omega, rows_out, gram_out,
    act, grads, act2, act_t, sk, ext, slab, send1, recv1, send2, recv2,
    send3, recv3, send4, recv4, part2, recv5,
    gram, recv6, full, recv7, quarter, recv8, ssem, rsem, lsem,
):
    layers, _, frames, height, width, channels = act_in.shape
    rank = omega.shape[1]
    dp, space = lax.axis_index("dp"), lax.axis_index("space")
    y, core = dp // 2, dp % 2
    x, z = space // RING, space % RING
    other_dp = y * 2 + 1 - core

    def along(axis, step):
        if axis == "x":
            return {"dp": dp, "space": (x + step) % RING * RING + z}
        if axis == "z":
            return {"dp": dp, "space": x * RING + (z + step) % RING}
        return {"dp": (y + step) % RING * 2 + core, "space": space}

    partner = {"dp": other_dp, "space": space}
    spaces = RING * RING
    below, above = (space + 1) % spaces, (space + spaces - 1) % spaces
    halo = [{"dp": dp, "space": at} for at in (below, above)]
    peers = [partner] + halo + [along(a, j) for a in ("x", "y", "z") for j in (1, 2, 3)]

    barrier = pltpu.get_barrier_semaphore()
    for peer in peers:
        pl.semaphore_signal(barrier, inc=1, device_id=peer, device_id_type=MESH)

    loads = []
    for l in range(layers):
        pair = [
            pltpu.make_async_copy(grads_in.at[l], grads.at[l], lsem.at[2 * l]),
            pltpu.make_async_copy(act_in.at[l], act.at[l], lsem.at[2 * l + 1]),
        ]
        for copy in pair:
            copy.start()
        loads.append(pair)
    pl.semaphore_wait(barrier, len(peers))

    sent = []

    def send(src, dst, to):
        at = len(sent)
        copy = pltpu.make_async_remote_copy(
            src_ref=src, dst_ref=dst, send_sem=ssem.at[at], recv_sem=rsem.at[at],
            device_id=to, device_id_type=MESH,
        )
        copy.start()
        sent.append(copy)
        return copy

    act_copies, halo_copies, row_copies = [], [], []
    for l in range(layers):
        loads[l][0].wait()
        for h in range(height):
            flat = grads[l, 0, :, h].reshape(frames * width, channels)
            value = jnp.dot(flat, omega[...], preferred_element_type=F32).astype(BF16)
            sk[l, 0, 1 + h] = value.reshape(frames, width, rank)
        halo_copies.append([
            send(sk.at[l, 0, height], sk.at[l, 0, 0], halo[0]),
            send(sk.at[l, 0, 1], sk.at[l, 0, height + 1], halo[1]),
        ])
        row_copies.append(send(sk.at[l, 0, 1:1 + height], sk.at[l, 1, 1:1 + height], partner))
        act_copies.append(send(act_in.at[l], act2.at[l], partner))

    def transpose(l, slot, source):
        for h in range(height):
            flat = source[l, 0, :, h].reshape(frames * width, channels)
            at = (slot * height + h) * frames * width
            act_t[l, :, at:at + frames * width] = flat.T

    column = lax.broadcasted_iota(jnp.int32, (frames * width, rank), 0) % width

    def extend(l, slot, h):
        value = sk[l, slot, h].reshape(frames * width, rank).astype(F32)
        if h == 0:
            value = jnp.where(space > 0, value, 0.0)
        if h == height + 1:
            value = jnp.where(space < spaces - 1, value, 0.0)
        ahead = jnp.where(column < width - 1, pltpu.roll(value, frames * width - 1, 0), 0.0)
        behind = jnp.where(column > 0, pltpu.roll(value, 1, 0), 0.0)
        for c, shifted in enumerate((ahead, value, behind)):
            zero = jnp.zeros((width, rank), BF16)
            ext[l, c, slot, h, 0] = zero
            ext[l, c, slot, h, frames + 1] = zero
            ext[l, c, slot, h, 1:1 + frames] = shifted.astype(BF16).reshape(frames, width, rank)

    inner, outer = range(1, 1 + height), (0, height + 1)

    def prepare_own(l):
        loads[l][1].wait()
        transpose(l, 0, act)
        for h in inner:
            extend(l, 0, h)

    def prepare_partner(l):
        row_copies[l].wait_recv()
        for h in inner:
            extend(l, 1, h)
        act_copies[l].wait_recv()
        transpose(l, 1, act2)

    relayed = []

    def relay(l):
        for copy in halo_copies[l]:
            copy.wait_recv()
        relayed.append([send(sk.at[l, 0, h], sk.at[l, 1, h], partner) for h in outer])
        for h in outer:
            extend(l, 0, h)

    def prepare_edges(l):
        for copy in relayed[l]:
            copy.wait_recv()
        for h in outer:
            extend(l, 1, h)

    prepare_own(0)
    prepare_partner(0)
    prepare_own(1)
    relay(0)
    prepare_edges(0)

    depth = 2 * height * frames * width

    def compute(n, r, l):
        owner = (y + r) % RING * 2 + core
        first = 27 * owner // 8

        def columns(k):
            k = jnp.minimum(first + k, 26)
            a, b, c = k // 9, k // 3 % 3, k % 3
            return ext[l, c, :, pl.ds(2 - b, height), pl.ds(2 - a, frames)].reshape(depth, rank)

        def pair(i, _):
            both = jnp.concatenate([columns(2 * i), columns(2 * i + 1)], axis=1)
            for m in range(3):
                rows = channels // 3
                value = jnp.dot(act_t[l, m * rows:(m + 1) * rows], both, preferred_element_type=F32)
                for s in range(2):
                    at = pl.multiple_of((2 * i + s) * channels + m * rows, rows)
                    slab[n, pl.ds(at, rows)] = value[:, s * rank:(s + 1) * rank]
            return 0

        lax.fori_loop(0, SLAB // 2, pair, 0)

    def window(n, r, l, mine, other):
        owner = (y + r) % RING * 2 + core
        place = mine * RING + other if l == 0 else other * RING + mine
        at = 27 * owner % 8 * (channels // 8) + OWN * place // 16 * 16
        return slab[n, pl.ds(pl.multiple_of(at, 16), WIN)]

    first_axis = ("x", "z")
    last_axis = ("z", "x")
    first_at = (x, z)
    last_at = (z, x)
    half1 = RING // 2
    step1, step2, step3, step4, step5 = {}, {}, {}, {}, {}

    def start1(n):
        r, l = CHUNKS[n]
        for o in range(RING):
            send1[n, o] = window(n, r, l, (first_at[l] + 2) % RING, o).astype(BF16)
        step1[n] = [
            send(send1.at[n, :half1], recv1.at[n, :half1], along(first_axis[l], 1)),
            send(send1.at[n, half1:], recv1.at[n, half1:], along(first_axis[l], 3)),
        ]

    def start2(n):
        r, l = CHUNKS[n]
        copies = []
        for s, step in enumerate((1, 3)):
            step1[n][s].wait_recv()
            for o in range(RING):
                value = window(n, r, l, (first_at[l] + step) % RING, o)
                if (o < half1) == (s == 0):
                    value = value + recv1[n, o].astype(F32)
                send2[n, s, o] = value.astype(BF16)
            copies.append(send(send2.at[n, s], recv2.at[n, s], along(first_axis[l], step)))
        step2[n] = copies

    def finish1(n):
        r, l = CHUNKS[n]
        for copy in step2[n]:
            copy.wait_recv()
        if r in (1, 3):
            step3[l][0 if r == 1 else 1].wait_recv()
        if r == 0:
            for copy in step4[l]:
                copy.wait_recv()
        for o in range(RING):
            value = window(n, r, l, first_at[l], o)
            value = value + recv2[n, 0, o].astype(F32) + recv2[n, 1, o].astype(F32)
            if r == 2:
                send3[l, o] = value.astype(STAGE2)
            elif r == 0:
                part2[l, o] = value + recv4[l, 0, o].astype(F32) + recv4[l, 1, o].astype(F32)
            else:
                s = 0 if r == 1 else 1
                if (o < half1) == (s == 0):
                    value = value + recv3[l, o].astype(F32)
                send4[l, s, o] = value.astype(STAGE2)
        if r == 2:
            step3[l] = [
                send(send3.at[l, :half1], recv3.at[l, :half1], along("y", 1)),
                send(send3.at[l, half1:], recv3.at[l, half1:], along("y", 3)),
            ]
        elif r == 0:
            step5[l] = [
                send(part2.at[l, (last_at[l] + j) % RING], recv5.at[l, j - 1], along(last_axis[l], j))
                for j in (1, 2, 3)
            ]
        else:
            s = 0 if r == 1 else 1
            step4.setdefault(l, []).append(send(send4.at[l, s], recv4.at[l, s], along("y", r)))

    total = len(CHUNKS)
    for n in range(total + LAG3):
        if n == 1:
            relay(1)
            prepare_partner(1)
            prepare_edges(1)
        if n < total:
            compute(n, *CHUNKS[n])
            start1(n)
        if LAG2 <= n < total + LAG2:
            start2(n - LAG2)
        if n >= LAG3:
            finish1(n - LAG3)

    shift = 2 * space % 16
    row = lax.broadcasted_iota(jnp.int32, (WIN, rank), 0)
    for l in range(layers):
        for copy in step5[l]:
            copy.wait_recv()
        value = part2[l, last_at[l]] + recv5[l, 0] + recv5[l, 1] + recv5[l, 2]
        value = pltpu.roll(value, (WIN - shift) % WIN, 0)
        value = jnp.where(row < OWN, value, 0.0)
        rows_out[l] = value
        gram[l] = lax.dot_general(
            value, value, (((0,), (0,)), ((), ())), precision=HIGHEST, preferred_element_type=F32
        )

    copy = send(gram.at[1 - core], recv6, partner)
    copy.wait_recv()
    full[0] = gram[core] + recv6[...]
    part = rank // RING

    def rows_of(step):
        return pl.ds(pl.multiple_of((y + step) % RING * part, part), part)

    copies = [send(full.at[0, rows_of(j)], recv7.at[j - 1], along("y", j)) for j in (1, 2, 3)]
    for copy in copies:
        copy.wait_recv()
    quarter[0] = full[0, rows_of(0)] + recv7[0] + recv7[1] + recv7[2]
    for s, axis in enumerate(("x", "z")):
        copies = [send(quarter.at[s], recv8.at[s, j - 1], along(axis, j)) for j in (1, 2, 3)]
        for copy in copies:
            copy.wait_recv()
        quarter[s + 1] = quarter[s] + recv8[s, 0] + recv8[s, 1] + recv8[s, 2]
    copies = [send(quarter.at[2], full.at[1, rows_of(0)], along("y", j)) for j in (1, 2, 3)]
    full[1, rows_of(0)] = quarter[2]
    for copy in copies:
        copy.wait_recv()
    copy = send(full.at[1], gram_out.at[core], partner)
    gram_out[core] = full[1]
    copy.wait_recv()
    for copy in sent:
        copy.wait_send()


def factor_kernel(rows, gram, out, work, inverse, *, scale):
    layers, rank, _ = gram.shape
    lane = lax.broadcasted_iota(jnp.int32, (PANEL, rank), 1)
    row = lax.broadcasted_iota(jnp.int32, (PANEL, rank), 0)
    wide = lax.broadcasted_iota(jnp.int32, (rank, rank), 1)
    work[...] = gram[...]
    for p in range(rank // PANEL):
        first = p * PANEL
        for l in range(layers):
            panel = work[l, first:first + PANEL]
            cols = [
                jnp.broadcast_to(panel[:, first + j:first + j + 1], (PANEL, rank)) for j in range(PANEL)
            ]
            pivots = jnp.ones((PANEL, rank), F32)
            for j in range(PANEL):
                pivot = jnp.broadcast_to(cols[j][j:j + 1], (PANEL, rank))
                pivots = jnp.where(row == j, pivot, pivots)
                if j < PANEL - 1:
                    mult = jnp.where(row > j, cols[j] / pivot, 0.0)
                    updated = panel - mult * panel[j:j + 1]
                    panel = jnp.where((lane == first + j) & (row > j), -mult, updated)
                    for i in range(j + 1, PANEL):
                        cols[i] = cols[i] - mult * cols[i][j:j + 1]
            inside = (lane >= first) & (lane < first + PANEL)
            unit = jnp.where(lane - first < row, panel, jnp.where(lane - first == row, 1.0, 0.0))
            full = jnp.where(inside, unit, panel)
            inverse[l, first:first + PANEL] = jnp.where(lane - first <= row, full, 0.0) / jnp.sqrt(pivots)
            if first + PANEL < rank:
                step = lax.dot_general(
                    panel / pivots, full, (((0,), (0,)), ((), ())),
                    precision=HIGHEST, preferred_element_type=F32,
                )
                rest = first + PANEL
                in_wide = (wide[rest:] >= first) & (wide[rest:] < rest)
                work[l, rest:] = jnp.where(in_wide, 0.0, work[l, rest:]) - step[rest:]
    for l in range(layers):
        value = lax.dot_general(
            rows[l], inverse[l], (((1,), (1,)), ((), ())),
            precision=HIGHEST, preferred_element_type=F32,
        )
        out[l] = (value * scale)[:OWN]


def shards(activations, out_grads, omega):
    layers, clips, frames, height, width, channels = activations.shape
    rank = omega.shape[1]
    chunks = len(CHUNKS)
    vmem = pl.BlockSpec(memory_space=pltpu.VMEM)
    blocks = (RING, WIN, rank)
    rows, gram = pl.pallas_call(
        reduce_kernel,
        name="reduce",
        out_shape=(
            jax.ShapeDtypeStruct((layers, WIN, rank), F32),
            jax.ShapeDtypeStruct((layers, rank, rank), F32),
        ),
        in_specs=[pl.BlockSpec(memory_space=pl.ANY)] * 2 + [vmem],
        out_specs=(vmem, vmem),
        scratch_shapes=[
            pltpu.VMEM(activations.shape, BF16),
            pltpu.VMEM(activations.shape, BF16),
            pltpu.VMEM(activations.shape, BF16),
            pltpu.VMEM((layers, channels, 2 * height * frames * width), BF16),
            pltpu.VMEM((layers, 2, height + 2, frames, width, rank), BF16),
            pltpu.VMEM((layers, 3, 2, height + 2, frames + 2, width, rank), BF16),
            pltpu.VMEM((chunks, SLAB * channels, rank), F32),
            pltpu.VMEM((chunks,) + blocks, BF16),
            pltpu.VMEM((chunks,) + blocks, BF16),
            pltpu.VMEM((chunks, 2) + blocks, BF16),
            pltpu.VMEM((chunks, 2) + blocks, BF16),
            pltpu.VMEM((layers,) + blocks, STAGE2),
            pltpu.VMEM((layers,) + blocks, STAGE2),
            pltpu.VMEM((layers, 2) + blocks, STAGE2),
            pltpu.VMEM((layers, 2) + blocks, STAGE2),
            pltpu.VMEM((layers,) + blocks, F32),
            pltpu.VMEM((layers, 3, WIN, rank), F32),
            pltpu.VMEM((layers, rank, rank), F32),
            pltpu.VMEM((rank, rank), F32),
            pltpu.VMEM((2, rank, rank), F32),
            pltpu.VMEM((3, rank // RING, rank), F32),
            pltpu.VMEM((3, rank // RING, rank), F32),
            pltpu.VMEM((2, 3, rank // RING, rank), F32),
            pltpu.SemaphoreType.DMA((80,)),
            pltpu.SemaphoreType.DMA((80,)),
            pltpu.SemaphoreType.DMA((2 * layers,)),
        ],
        compiler_params=pltpu.CompilerParams(
            collective_id=0, has_side_effects=True, vmem_limit_bytes=60 * 2**20
        ),
    )(activations, out_grads, omega)
    return pl.pallas_call(
        functools.partial(factor_kernel, scale=math.sqrt(27 * channels)),
        name="factor",
        out_shape=jax.ShapeDtypeStruct((layers, OWN, rank), F32),
        in_specs=[vmem] * 2,
        out_specs=vmem,
        scratch_shapes=[
            pltpu.VMEM((layers, rank, rank), F32),
            pltpu.VMEM((layers, rank, rank), F32),
        ],
    )(rows, gram)


def solution(mesh):
    return jax.shard_map(
        shards,
        mesh=mesh,
        in_specs=(
            P(None, "dp", None, "space", None, None),
            P(None, "dp", None, "space", None, None),
            P(),
        ),
        out_specs=P(None, ("dp", "space"), None),
        check_vma=False,
    )
```

```python
import functools
import math

import jax
import jax.numpy as jnp
from jax import lax
from jax.experimental import pallas as pl
from jax.experimental.pallas import tpu as pltpu
from jax.sharding import PartitionSpec as P

MESH = pl.DeviceIdType.MESH
BF16, F32 = jnp.bfloat16, jnp.float32
HIGHEST = lax.Precision.HIGHEST
RING = 4
OWN = 162
WIN = 176
BLOCK = OWN * 16
SLAB = 6
ORDER = (2, 1, 3, 0)
CHUNKS = [(r, l) for r in ORDER for l in (0, 1)]
PANEL = 16
LAG2, LAG3 = 2, 4
STAGE2 = BF16


def reduce_kernel(
    act_in, grads_in, omega, rows_out, gram_out,
    act, grads, act2, act_t, sk, ext, slab, send1, recv1, send2, recv2,
    send3, recv3, send4, recv4, part2, recv5,
    gram, recv6, part, recv7, ssem, rsem, lsem,
):
    layers, _, frames, height, width, channels = act_in.shape
    rank = omega.shape[1]
    dp, space = lax.axis_index("dp"), lax.axis_index("space")
    y, core = dp // 2, dp % 2
    x, z = space // RING, space % RING
    other_dp = y * 2 + 1 - core

    def along(axis, step):
        if axis == "x":
            return {"dp": dp, "space": (x + step) % RING * RING + z}
        if axis == "z":
            return {"dp": dp, "space": x * RING + (z + step) % RING}
        return {"dp": (y + step) % RING * 2 + core, "space": space}

    partner = {"dp": other_dp, "space": space}
    spaces = RING * RING
    below, above = (space + 1) % spaces, (space + spaces - 1) % spaces
    halo = [{"dp": dp, "space": at} for at in (below, above)]
    turns = [(a, b) for a in range(RING) for b in range(RING) if a or b]
    plane = [
        {"dp": dp, "space": (x + a) % RING * RING + (z + b) % RING} for a, b in turns
    ]
    column_turns = [(a, c) for a in range(RING) for c in range(2) if a or c]
    stack = [
        {"dp": (y + a) % RING * 2 + (core + c) % 2, "space": space} for a, c in column_turns
    ]
    peers = plane + stack

    barrier = pltpu.get_barrier_semaphore()
    for peer in peers:
        pl.semaphore_signal(barrier, inc=1, device_id=peer, device_id_type=MESH)

    loads = []
    for l in range(layers):
        pair = [
            pltpu.make_async_copy(grads_in.at[l], grads.at[l], lsem.at[2 * l]),
            pltpu.make_async_copy(act_in.at[l], act.at[l], lsem.at[2 * l + 1]),
        ]
        for copy in pair:
            copy.start()
        loads.append(pair)
    pl.semaphore_wait(barrier, len(peers))

    sent = []

    def send(src, dst, to):
        at = len(sent)
        copy = pltpu.make_async_remote_copy(
            src_ref=src, dst_ref=dst, send_sem=ssem.at[at], recv_sem=rsem.at[at],
            device_id=to, device_id_type=MESH,
        )
        copy.start()
        sent.append(copy)
        return copy

    act_copies, halo_copies, row_copies = [], [], []
    for l in range(layers):
        loads[l][0].wait()
        for h in range(height):
            flat = grads[l, 0, :, h].reshape(frames * width, channels)
            value = jnp.dot(flat, omega[...], preferred_element_type=F32).astype(BF16)
            sk[l, 0, 1 + h] = value.reshape(frames, width, rank)
        halo_copies.append([
            send(sk.at[l, 0, height], sk.at[l, 0, 0], halo[0]),
            send(sk.at[l, 0, 1], sk.at[l, 0, height + 1], halo[1]),
        ])
        row_copies.append(send(sk.at[l, 0, 1:1 + height], sk.at[l, 1, 1:1 + height], partner))
        act_copies.append(send(act_in.at[l], act2.at[l], partner))

    def transpose(l, slot, source):
        for h in range(height):
            flat = source[l, 0, :, h].reshape(frames * width, channels)
            at = (slot * height + h) * frames * width
            act_t[l, :, at:at + frames * width] = flat.T

    column = lax.broadcasted_iota(jnp.int32, (frames * width, rank), 0) % width

    def extend(l, slot, h):
        value = sk[l, slot, h].reshape(frames * width, rank).astype(F32)
        if h == 0:
            value = jnp.where(space > 0, value, 0.0)
        if h == height + 1:
            value = jnp.where(space < spaces - 1, value, 0.0)
        ahead = jnp.where(column < width - 1, pltpu.roll(value, frames * width - 1, 0), 0.0)
        behind = jnp.where(column > 0, pltpu.roll(value, 1, 0), 0.0)
        for c, shifted in enumerate((ahead, value, behind)):
            zero = jnp.zeros((width, rank), BF16)
            ext[l, c, slot, h, 0] = zero
            ext[l, c, slot, h, frames + 1] = zero
            ext[l, c, slot, h, 1:1 + frames] = shifted.astype(BF16).reshape(frames, width, rank)

    inner, outer = range(1, 1 + height), (0, height + 1)

    def prepare_own(l):
        loads[l][1].wait()
        transpose(l, 0, act)
        for h in inner:
            extend(l, 0, h)

    def prepare_partner(l):
        row_copies[l].wait_recv()
        for h in inner:
            extend(l, 1, h)
        act_copies[l].wait_recv()
        transpose(l, 1, act2)

    relayed = []

    def relay(l):
        for copy in halo_copies[l]:
            copy.wait_recv()
        relayed.append([send(sk.at[l, 0, h], sk.at[l, 1, h], partner) for h in outer])
        for h in outer:
            extend(l, 0, h)

    def prepare_edges(l):
        for copy in relayed[l]:
            copy.wait_recv()
        for h in outer:
            extend(l, 1, h)

    prepare_own(0)
    prepare_partner(0)
    prepare_own(1)
    relay(0)
    prepare_edges(0)

    depth = 2 * height * frames * width

    def compute(n, r, l):
        owner = (y + r) % RING * 2 + core
        first = 27 * owner // 8

        def columns(k):
            k = jnp.minimum(first + k, 26)
            a, b, c = k // 9, k // 3 % 3, k % 3
            return ext[l, c, :, pl.ds(2 - b, height), pl.ds(2 - a, frames)].reshape(depth, rank)

        def pair(i, _):
            both = jnp.concatenate([columns(2 * i), columns(2 * i + 1)], axis=1)
            for m in range(3):
                rows = channels // 3
                value = jnp.dot(act_t[l, m * rows:(m + 1) * rows], both, preferred_element_type=F32)
                for s in range(2):
                    at = pl.multiple_of((2 * i + s) * channels + m * rows, rows)
                    slab[n, pl.ds(at, rows)] = value[:, s * rank:(s + 1) * rank]
            return 0

        lax.fori_loop(0, SLAB // 2, pair, 0)

    def window(n, r, l, mine, other):
        owner = (y + r) % RING * 2 + core
        place = mine * RING + other if l == 0 else other * RING + mine
        at = 27 * owner % 8 * (channels // 8) + OWN * place // 16 * 16
        return slab[n, pl.ds(pl.multiple_of(at, 16), WIN)]

    first_axis = ("x", "z")
    last_axis = ("z", "x")
    first_at = (x, z)
    last_at = (z, x)
    half1 = RING // 2
    step1, step2, step3, step4, step5 = {}, {}, {}, {}, {}

    def start1(n):
        r, l = CHUNKS[n]
        for o in range(RING):
            send1[n, o] = window(n, r, l, (first_at[l] + 2) % RING, o).astype(BF16)
        step1[n] = [
            send(send1.at[n, :half1], recv1.at[n, :half1], along(first_axis[l], 1)),
            send(send1.at[n, half1:], recv1.at[n, half1:], along(first_axis[l], 3)),
        ]

    def start2(n):
        r, l = CHUNKS[n]
        copies = []
        for s, step in enumerate((1, 3)):
            step1[n][s].wait_recv()
            for o in range(RING):
                value = window(n, r, l, (first_at[l] + step) % RING, o)
                if (o < half1) == (s == 0):
                    value = value + recv1[n, o].astype(F32)
                send2[n, s, o] = value.astype(BF16)
            copies.append(send(send2.at[n, s], recv2.at[n, s], along(first_axis[l], step)))
        step2[n] = copies

    def finish1(n):
        r, l = CHUNKS[n]
        for copy in step2[n]:
            copy.wait_recv()
        if r in (1, 3):
            step3[l][0 if r == 1 else 1].wait_recv()
        if r == 0:
            for copy in step4[l]:
                copy.wait_recv()
        for o in range(RING):
            value = window(n, r, l, first_at[l], o)
            value = value + recv2[n, 0, o].astype(F32) + recv2[n, 1, o].astype(F32)
            if r == 2:
                send3[l, o] = value.astype(STAGE2)
            elif r == 0:
                part2[l, o] = value + recv4[l, 0, o].astype(F32) + recv4[l, 1, o].astype(F32)
            else:
                s = 0 if r == 1 else 1
                if (o < half1) == (s == 0):
                    value = value + recv3[l, o].astype(F32)
                send4[l, s, o] = value.astype(STAGE2)
        if r == 2:
            step3[l] = [
                send(send3.at[l, :half1], recv3.at[l, :half1], along("y", 1)),
                send(send3.at[l, half1:], recv3.at[l, half1:], along("y", 3)),
            ]
        elif r == 0:
            step5[l] = [
                send(part2.at[l, (last_at[l] + j) % RING], recv5.at[l, j - 1], along(last_axis[l], j))
                for j in (1, 2, 3)
            ]
        else:
            s = 0 if r == 1 else 1
            step4.setdefault(l, []).append(send(send4.at[l, s], recv4.at[l, s], along("y", r)))

    total = len(CHUNKS)
    for n in range(total + LAG3):
        if n == 1:
            relay(1)
            prepare_partner(1)
            prepare_edges(1)
        if n < total:
            compute(n, *CHUNKS[n])
            start1(n)
        if LAG2 <= n < total + LAG2:
            start2(n - LAG2)
        if n >= LAG3:
            finish1(n - LAG3)

    shift = 2 * space % 16
    row = lax.broadcasted_iota(jnp.int32, (WIN, rank), 0)
    for l in range(layers):
        for copy in step5[l]:
            copy.wait_recv()
        value = part2[l, last_at[l]] + recv5[l, 0] + recv5[l, 1] + recv5[l, 2]
        value = pltpu.roll(value, (WIN - shift) % WIN, 0)
        value = jnp.where(row < OWN, value, 0.0)
        rows_out[l] = value
        product = lax.dot_general(
            value, value, (((0,), (0,)), ((), ())), precision=HIGHEST, preferred_element_type=F32
        )
        gram[l * rank // 16:(l + 1) * rank // 16] = product.reshape(rank // 16, 16, rank)

    copies = [
        send(gram.at[to["space"]], recv6.at[n], to) for n, to in enumerate(plane)
    ]
    value = gram[space]
    for n, copy in enumerate(copies):
        copy.wait_recv()
        value = value + recv6[n]
    part[0] = value
    copies = [send(part.at[0], recv7.at[n], to) for n, to in enumerate(stack)]
    for n, copy in enumerate(copies):
        copy.wait_recv()
        value = value + recv7[n]
    part[1] = value
    gram_out[space] = value
    copies = [send(part.at[1], gram_out.at[space], to) for to in plane]
    for copy in copies:
        copy.wait_recv()
    for copy in sent:
        copy.wait_send()


def factor_kernel(rows, gram, out, work, inverse, *, scale):
    layers, rank, _ = gram.shape
    lane = lax.broadcasted_iota(jnp.int32, (PANEL, rank), 1)
    row = lax.broadcasted_iota(jnp.int32, (PANEL, rank), 0)
    wide = lax.broadcasted_iota(jnp.int32, (rank, rank), 1)
    work[...] = gram[...]
    for p in range(rank // PANEL):
        first = p * PANEL
        rest = first + PANEL
        at = lane - first
        for l in range(layers):
            lower = work[l, first:rest]
            solved = lower
            cols = [
                jnp.broadcast_to(lower[:, first + j:first + j + 1], (PANEL, rank)) for j in range(PANEL)
            ]
            roots = jnp.ones((PANEL, rank), F32)
            for j in range(PANEL):
                own = row == j
                pivot = jnp.broadcast_to(cols[j][j:j + 1], (PANEL, rank))
                roots = jnp.where(own, pivot, roots)
                scaled = 1.0 / pivot
                mult = cols[j] * scaled
                for i in range(j + 1, PANEL):
                    line = jnp.broadcast_to(cols[i][j:j + 1], (PANEL, rank))
                    cols[i] = jnp.where(own, line * scaled, cols[i] - mult * line)
                line = jnp.broadcast_to(solved[j:j + 1], (PANEL, rank))
                pick = jnp.where(own, scaled, -mult)
                solved = jnp.where(at == j, pick, jnp.where(own, line * scaled, solved - mult * line))
                below = jnp.where(row > j, mult, 0.0)
                updated = lower - below * lower[j:j + 1]
                lower = jnp.where((at == j) & (row > j), -mult, updated)
            lower = jnp.where(at < row, lower, jnp.where(at == row, 1.0, 0.0))
            inverse[l, first:rest] = lower / jnp.sqrt(roots)
            if rest < rank:
                parts = [jnp.zeros((first, rank), F32)] if first else []
                parts += [solved, jnp.zeros((rank - rest, rank), F32)]
                left = work[l, rest:]
                step = jnp.dot(
                    left, jnp.concatenate(parts, axis=0), precision=HIGHEST, preferred_element_type=F32
                )
                inside = (wide[rest:] >= first) & (wide[rest:] < rest)
                work[l, rest:] = jnp.where(inside, 0.0, left) - step
    for l in range(layers):
        value = lax.dot_general(
            rows[l], inverse[l], (((1,), (1,)), ((), ())),
            precision=HIGHEST, preferred_element_type=F32,
        )
        out[:, l] = (value * scale)[:OWN]


def shards(activations, out_grads, omega):
    layers, clips, frames, height, width, channels = activations.shape
    rank = omega.shape[1]
    chunks = len(CHUNKS)
    vmem = pl.BlockSpec(memory_space=pltpu.VMEM)
    blocks = (RING, WIN, rank)
    rows, gram = pl.pallas_call(
        reduce_kernel,
        name="reduce",
        out_shape=(
            jax.ShapeDtypeStruct((layers, WIN, rank), F32),
            jax.ShapeDtypeStruct((RING * RING, 16, rank), F32),
        ),
        in_specs=[pl.BlockSpec(memory_space=pl.ANY)] * 2 + [vmem],
        out_specs=(vmem, vmem),
        scratch_shapes=[
            pltpu.VMEM(activations.shape, BF16),
            pltpu.VMEM(activations.shape, BF16),
            pltpu.VMEM(activations.shape, BF16),
            pltpu.VMEM((layers, channels, 2 * height * frames * width), BF16),
            pltpu.VMEM((layers, 2, height + 2, frames, width, rank), BF16),
            pltpu.VMEM((layers, 3, 2, height + 2, frames + 2, width, rank), BF16),
            pltpu.VMEM((chunks, SLAB * channels, rank), F32),
            pltpu.VMEM((chunks,) + blocks, BF16),
            pltpu.VMEM((chunks,) + blocks, BF16),
            pltpu.VMEM((chunks, 2) + blocks, BF16),
            pltpu.VMEM((chunks, 2) + blocks, BF16),
            pltpu.VMEM((layers,) + blocks, STAGE2),
            pltpu.VMEM((layers,) + blocks, STAGE2),
            pltpu.VMEM((layers, 2) + blocks, STAGE2),
            pltpu.VMEM((layers, 2) + blocks, STAGE2),
            pltpu.VMEM((layers,) + blocks, F32),
            pltpu.VMEM((layers, 3, WIN, rank), F32),
            pltpu.VMEM((RING * RING, 16, rank), F32),
            pltpu.VMEM((RING * RING - 1, 16, rank), F32),
            pltpu.VMEM((2, 16, rank), F32),
            pltpu.VMEM((2 * RING - 1, 16, rank), F32),
            pltpu.SemaphoreType.DMA((112,)),
            pltpu.SemaphoreType.DMA((112,)),
            pltpu.SemaphoreType.DMA((2 * layers,)),
        ],
        compiler_params=pltpu.CompilerParams(
            collective_id=0, has_side_effects=True, vmem_limit_bytes=60 * 2**20
        ),
    )(activations, out_grads, omega)
    basis = pl.pallas_call(
        functools.partial(factor_kernel, scale=math.sqrt(27 * channels)),
        name="factor",
        out_shape=jax.ShapeDtypeStruct((OWN, layers, rank), F32),
        in_specs=[vmem] * 2,
        out_specs=vmem,
        scratch_shapes=[
            pltpu.VMEM((layers, rank, rank), F32),
            pltpu.VMEM((layers, rank, rank), F32),
        ],
    )(rows, gram.reshape(layers, rank, rank))
    return jnp.transpose(basis, (1, 0, 2))


def solution(mesh):
    return jax.shard_map(
        shards,
        mesh=mesh,
        in_specs=(
            P(None, "dp", None, "space", None, None),
            P(None, "dp", None, "space", None, None),
            P(),
        ),
        out_specs=P(None, ("dp", "space"), None),
        check_vma=False,
    )
```

```python
import functools
import math

import jax
import jax.numpy as jnp
from jax import lax
from jax.experimental import pallas as pl
from jax.experimental.pallas import tpu as pltpu
from jax.sharding import PartitionSpec as P

MESH = pl.DeviceIdType.MESH
BF16, F32 = jnp.bfloat16, jnp.float32
HIGHEST = lax.Precision.HIGHEST
RING = 4
OWN = 162
WIN = 176
BLOCK = OWN * 16
SLAB = 8
ORDER = (2, 1, 3, 0)
CHUNKS = [(r, e) for r in ORDER for e in (0, 1)]
PANEL = 16
LAG2, LAG3 = 2, 4
STAGE2 = BF16


def reduce_kernel(
    act_in, grads_in, omega, rows_out, gram_out,
    act, grads, act2, act_t, other, sk, ext, slab, send1, recv1, send2, recv2,
    send3, recv3, send4, recv4, part2, recv5, rolled,
    gram, recv6, part, recv7, full, ssem, rsem, lsem,
):
    layers, _, frames, height, width, channels = act_in.shape
    rank = omega.shape[1]
    dp, space = lax.axis_index("dp"), lax.axis_index("space")
    y, core = dp // 2, dp % 2
    x, z = space // RING, space % RING
    other_dp = y * 2 + 1 - core

    def along(axis, step):
        if axis == "x":
            return {"dp": dp, "space": (x + step) % RING * RING + z}
        if axis == "z":
            return {"dp": dp, "space": x * RING + (z + step) % RING}
        return {"dp": (y + step) % RING * 2 + core, "space": space}

    partner = {"dp": other_dp, "space": space}
    spaces = RING * RING
    below, above = (space + 1) % spaces, (space + spaces - 1) % spaces
    turns = [(a, b) for a in range(RING) for b in range(RING) if a or b]
    plane = [
        {"dp": dp, "space": (x + a) % RING * RING + (z + b) % RING} for a, b in turns
    ]
    stack = [along("y", j) for j in (1, 2, 3)]
    crossed = [{"dp": other_dp, "space": below}, {"dp": other_dp, "space": above}]
    peers = [partner] + crossed + plane + stack

    barrier = pltpu.get_barrier_semaphore()
    for peer in peers:
        pl.semaphore_signal(barrier, inc=1, device_id=peer, device_id_type=MESH)

    loads = [
        pltpu.make_async_copy(grads_in.at[1 - core], grads.at[0], lsem.at[0]),
        pltpu.make_async_copy(grads_in.at[core], grads.at[1], lsem.at[1]),
        pltpu.make_async_copy(act_in.at[core], act, lsem.at[2]),
    ]
    for copy in loads:
        copy.start()

    def sketch(n, h):
        flat = grads[n, 0, :, h].reshape(frames * width, channels)
        value = jnp.dot(flat, omega[...], preferred_element_type=F32).astype(BF16)
        return value.reshape(frames, width, rank)

    loads[0].wait()
    for h in range(height):
        other[h] = sketch(0, h)
    loads[1].wait()
    for h in range(height):
        sk[0, 1 + h] = sketch(1, h)

    pl.semaphore_wait(barrier, len(peers))
    sent = []

    def send(src, dst, to):
        at = len(sent)
        copy = pltpu.make_async_remote_copy(
            src_ref=src, dst_ref=dst, send_sem=ssem.at[at], recv_sem=rsem.at[at],
            device_id=to, device_id_type=MESH,
        )
        copy.start()
        sent.append(copy)
        return copy

    halo_copies = [
        [
            send(sk.at[0, height], sk.at[0, 0], {"dp": dp, "space": below}),
            send(sk.at[0, 1], sk.at[0, height + 1], {"dp": dp, "space": above}),
        ],
        [
            send(other.at[height - 1], sk.at[1, 0], crossed[0]),
            send(other.at[0], sk.at[1, height + 1], crossed[1]),
        ],
    ]
    row_copy = send(other, sk.at[1, 1:1 + height], partner)
    act_copy = send(act_in.at[1 - core], act2, partner)

    def transpose(slot, source):
        for h in range(height):
            flat = source[0, :, h].reshape(frames * width, channels)
            at = (slot * height + h) * frames * width
            act_t[:, at:at + frames * width] = flat.T

    column = lax.broadcasted_iota(jnp.int32, (frames * width, rank), 0) % width

    def extend(slot, h):
        value = sk[slot, h].reshape(frames * width, rank).astype(F32)
        if h == 0:
            value = jnp.where(space > 0, value, 0.0)
        if h == height + 1:
            value = jnp.where(space < spaces - 1, value, 0.0)
        ahead = jnp.where(column < width - 1, pltpu.roll(value, frames * width - 1, 0), 0.0)
        behind = jnp.where(column > 0, pltpu.roll(value, 1, 0), 0.0)
        for c, shifted in enumerate((ahead, value, behind)):
            zero = jnp.zeros((width, rank), BF16)
            ext[c, slot, h, 0] = zero
            ext[c, slot, h, frames + 1] = zero
            ext[c, slot, h, 1:1 + frames] = shifted.astype(BF16).reshape(frames, width, rank)

    inner, outer = range(1, 1 + height), (0, height + 1)
    loads[2].wait()
    transpose(0, act)
    for h in inner:
        extend(0, h)
    row_copy.wait_recv()
    for h in inner:
        extend(1, h)
    act_copy.wait_recv()
    transpose(1, act2)
    for slot in range(2):
        for copy, h in zip(halo_copies[slot], outer):
            copy.wait_recv()
            extend(slot, h)

    depth = 2 * height * frames * width

    def compute(r, pairs):
        first = 27 * ((y + r) % RING * 2) // 8

        def columns(k):
            k = jnp.minimum(first + k, 26)
            a, b, c = k // 9, k // 3 % 3, k % 3
            return ext[c, :, pl.ds(2 - b, height), pl.ds(2 - a, frames)].reshape(depth, rank)

        def pair(i, _):
            both = jnp.concatenate([columns(2 * i), columns(2 * i + 1)], axis=1)
            for m in range(3):
                rows = channels // 3
                value = jnp.dot(act_t[m * rows:(m + 1) * rows], both, preferred_element_type=F32)
                for s in range(2):
                    at = pl.multiple_of((2 * i + s) * channels + m * rows, rows)
                    slab[r, pl.ds(at, rows)] = value[:, s * rank:(s + 1) * rank]
            return 0

        lax.fori_loop(pairs[0], pairs[1], pair, 0)

    def window(r, e, mine, o):
        owner = (y + r) % RING * 2 + e
        place = mine * RING + o if e == 0 else o * RING + mine
        start = 27 * owner - 27 * (owner - e) // 8 * 8
        at = start * (channels // 8) + OWN * place // 16 * 16
        return slab[r, pl.ds(pl.multiple_of(at, 16), WIN)]

    first_axis = ("x", "z")
    last_axis = ("z", "x")
    first_at = (x, z)
    last_at = (z, x)
    half1 = RING // 2
    step1, step2, step3, step4, step5 = {}, {}, {}, {}, {}

    def start1(n):
        r, e = CHUNKS[n]
        for o in range(RING):
            send1[n, o] = window(r, e, (first_at[e] + 2) % RING, o).astype(BF16)
        step1[n] = [
            send(send1.at[n, :half1], recv1.at[n, :half1], along(first_axis[e], 1)),
            send(send1.at[n, half1:], recv1.at[n, half1:], along(first_axis[e], 3)),
        ]

    def start2(n):
        r, e = CHUNKS[n]
        copies = []
        for s, step in enumerate((1, 3)):
            step1[n][s].wait_recv()
            for o in range(RING):
                value = window(r, e, (first_at[e] + step) % RING, o)
                if (o < half1) == (s == 0):
                    value = value + recv1[n, o].astype(F32)
                send2[n, s, o] = value.astype(BF16)
            copies.append(send(send2.at[n, s], recv2.at[n, s], along(first_axis[e], step)))
        step2[n] = copies

    def finish1(n):
        r, e = CHUNKS[n]
        for copy in step2[n]:
            copy.wait_recv()
        if r in (1, 3):
            step3[e][0 if r == 1 else 1].wait_recv()
        if r == 0:
            for copy in step4[e]:
                copy.wait_recv()
        for o in range(RING):
            value = window(r, e, first_at[e], o)
            value = value + recv2[n, 0, o].astype(F32) + recv2[n, 1, o].astype(F32)
            if r == 2:
                send3[e, o] = value.astype(STAGE2)
            elif r == 0:
                part2[e, o] = value + recv4[e, 0, o].astype(F32) + recv4[e, 1, o].astype(F32)
            else:
                s = 0 if r == 1 else 1
                if (o < half1) == (s == 0):
                    value = value + recv3[e, o].astype(F32)
                send4[e, s, o] = value.astype(STAGE2)
        if r == 2:
            step3[e] = [
                send(send3.at[e, :half1], recv3.at[e, :half1], along("y", 1)),
                send(send3.at[e, half1:], recv3.at[e, half1:], along("y", 3)),
            ]
        elif r == 0:
            step5[e] = [
                send(part2.at[e, (last_at[e] + j) % RING], recv5.at[e, j - 1], along(last_axis[e], j))
                for j in (1, 2, 3)
            ]
        else:
            s = 0 if r == 1 else 1
            step4.setdefault(e, []).append(send(send4.at[e, s], recv4.at[e, s], along("y", r)))

    total = len(CHUNKS)
    for n in range(total + LAG3):
        if n < total:
            r, e = CHUNKS[n]
            compute(r, ((0, 3), (3, 4))[e])
            start1(n)
        if LAG2 <= n < total + LAG2:
            start2(n - LAG2)
        if n >= LAG3:
            finish1(n - LAG3)

    shift = 2 * space % 16
    row = lax.broadcasted_iota(jnp.int32, (WIN, rank), 0)
    product = jnp.zeros((rank, rank), F32)
    for e in range(2):
        for copy in step5[e]:
            copy.wait_recv()
        value = part2[e, last_at[e]] + recv5[e, 0] + recv5[e, 1] + recv5[e, 2]
        value = pltpu.roll(value, (WIN - shift) % WIN, 0)
        value = jnp.where(row < OWN, value, 0.0)
        rolled[e] = value
        product = product + lax.dot_general(
            value, value, (((0,), (0,)), ((), ())), precision=HIGHEST, preferred_element_type=F32
        )
    gram[...] = product.reshape(spaces, rank // spaces, rank)

    copies = [send(gram.at[to["space"]], recv6.at[n], to) for n, to in enumerate(plane)]
    rows_copy = send(rolled.at[1 - core], rows_out.at[core], partner)
    rows_out[core] = rolled[core]
    value = gram[space]
    for n, copy in enumerate(copies):
        copy.wait_recv()
        value = value + recv6[n]
    part[0] = value
    copies = [send(part.at[0], recv7.at[n], to) for n, to in enumerate(stack)]
    for n, copy in enumerate(copies):
        copy.wait_recv()
        value = value + recv7[n]
    part[1] = value
    full[space] = value
    copies = [send(part.at[1], full.at[space], to) for to in plane]
    for copy in copies:
        copy.wait_recv()
    copy = send(full, gram_out.at[core], partner)
    gram_out[core] = full[...]
    copy.wait_recv()
    rows_copy.wait_recv()
    for copy in sent:
        copy.wait_send()


def factor_kernel(rows, gram, out, work, inverse, *, scale):
    layers, rank, _ = gram.shape
    lane = lax.broadcasted_iota(jnp.int32, (PANEL, rank), 1)
    row = lax.broadcasted_iota(jnp.int32, (PANEL, rank), 0)
    wide = lax.broadcasted_iota(jnp.int32, (rank, rank), 1)
    work[...] = gram[...]
    for p in range(rank // PANEL):
        first = p * PANEL
        rest = first + PANEL
        at = lane - first
        for l in range(layers):
            lower = work[l, first:rest]
            solved = lower
            cols = [
                jnp.broadcast_to(lower[:, first + j:first + j + 1], (PANEL, rank)) for j in range(PANEL)
            ]
            roots = jnp.ones((PANEL, rank), F32)
            for j in range(PANEL):
                own = row == j
                pivot = jnp.broadcast_to(cols[j][j:j + 1], (PANEL, rank))
                roots = jnp.where(own, pivot, roots)
                scaled = 1.0 / pivot
                mult = cols[j] * scaled
                for i in range(j + 1, PANEL):
                    line = jnp.broadcast_to(cols[i][j:j + 1], (PANEL, rank))
                    cols[i] = jnp.where(own, line * scaled, cols[i] - mult * line)
                line = jnp.broadcast_to(solved[j:j + 1], (PANEL, rank))
                pick = jnp.where(own, scaled, -mult)
                solved = jnp.where(at == j, pick, jnp.where(own, line * scaled, solved - mult * line))
                below = jnp.where(row > j, mult, 0.0)
                updated = lower - below * lower[j:j + 1]
                lower = jnp.where((at == j) & (row > j), -mult, updated)
            lower = jnp.where(at < row, lower, jnp.where(at == row, 1.0, 0.0))
            inverse[l, first:rest] = lower / jnp.sqrt(roots)
            if rest < rank:
                parts = [jnp.zeros((first, rank), F32)] if first else []
                parts += [solved, jnp.zeros((rank - rest, rank), F32)]
                left = work[l, rest:]
                step = jnp.dot(
                    left, jnp.concatenate(parts, axis=0), precision=HIGHEST, preferred_element_type=F32
                )
                inside = (wide[rest:] >= first) & (wide[rest:] < rest)
                work[l, rest:] = jnp.where(inside, 0.0, left) - step
    for l in range(layers):
        value = lax.dot_general(
            rows[l], inverse[l], (((1,), (1,)), ((), ())),
            precision=HIGHEST, preferred_element_type=F32,
        )
        out[:, l] = (value * scale)[:OWN]


def shards(activations, out_grads, omega):
    layers, clips, frames, height, width, channels = activations.shape
    rank = omega.shape[1]
    chunks = len(CHUNKS)
    vmem = pl.BlockSpec(memory_space=pltpu.VMEM)
    blocks = (RING, WIN, rank)
    gram_blocks = (RING * RING, rank // (RING * RING), rank)
    rows, gram = pl.pallas_call(
        reduce_kernel,
        name="reduce",
        out_shape=(
            jax.ShapeDtypeStruct((layers, WIN, rank), F32),
            jax.ShapeDtypeStruct((layers,) + gram_blocks, F32),
        ),
        in_specs=[pl.BlockSpec(memory_space=pl.ANY)] * 2 + [vmem],
        out_specs=(vmem, vmem),
        scratch_shapes=[
            pltpu.VMEM(activations.shape[1:], BF16),
            pltpu.VMEM(activations.shape, BF16),
            pltpu.VMEM(activations.shape[1:], BF16),
            pltpu.VMEM((channels, 2 * height * frames * width), BF16),
            pltpu.VMEM((height, frames, width, rank), BF16),
            pltpu.VMEM((2, height + 2, frames, width, rank), BF16),
            pltpu.VMEM((3, 2, height + 2, frames + 2, width, rank), BF16),
            pltpu.VMEM((RING, SLAB * channels, rank), F32),
            pltpu.VMEM((chunks,) + blocks, BF16),
            pltpu.VMEM((chunks,) + blocks, BF16),
            pltpu.VMEM((chunks, 2) + blocks, BF16),
            pltpu.VMEM((chunks, 2) + blocks, BF16),
            pltpu.VMEM((2,) + blocks, STAGE2),
            pltpu.VMEM((2,) + blocks, STAGE2),
            pltpu.VMEM((2, 2) + blocks, STAGE2),
            pltpu.VMEM((2, 2) + blocks, STAGE2),
            pltpu.VMEM((2,) + blocks, F32),
            pltpu.VMEM((2, 3, WIN, rank), F32),
            pltpu.VMEM((2, WIN, rank), F32),
            pltpu.VMEM(gram_blocks, F32),
            pltpu.VMEM((RING * RING - 1,) + gram_blocks[1:], F32),
            pltpu.VMEM((2,) + gram_blocks[1:], F32),
            pltpu.VMEM((RING - 1,) + gram_blocks[1:], F32),
            pltpu.VMEM(gram_blocks, F32),
            pltpu.SemaphoreType.DMA((112,)),
            pltpu.SemaphoreType.DMA((112,)),
            pltpu.SemaphoreType.DMA((3,)),
        ],
        compiler_params=pltpu.CompilerParams(
            collective_id=0, has_side_effects=True, vmem_limit_bytes=60 * 2**20
        ),
    )(activations, out_grads, omega)
    basis = pl.pallas_call(
        functools.partial(factor_kernel, scale=math.sqrt(27 * channels)),
        name="factor",
        out_shape=jax.ShapeDtypeStruct((OWN, layers, rank), F32),
        in_specs=[vmem] * 2,
        out_specs=vmem,
        scratch_shapes=[
            pltpu.VMEM((layers, rank, rank), F32),
            pltpu.VMEM((layers, rank, rank), F32),
        ],
    )(rows, gram.reshape(layers, rank, rank))
    return jnp.transpose(basis, (1, 0, 2))


def solution(mesh):
    return jax.shard_map(
        shards,
        mesh=mesh,
        in_specs=(
            P(None, "dp", None, "space", None, None),
            P(None, "dp", None, "space", None, None),
            P(),
        ),
        out_specs=P(None, ("dp", "space"), None),
        check_vma=False,
    )
```

```python
import functools
import math

import jax
import jax.numpy as jnp
from jax import lax
from jax.experimental import pallas as pl
from jax.experimental.pallas import tpu as pltpu
from jax.sharding import PartitionSpec as P

MESH = pl.DeviceIdType.MESH
BF16, F32 = jnp.bfloat16, jnp.float32
HIGHEST = lax.Precision.HIGHEST
RING = 4
OWN = 162
WIN = 176
BLOCK = OWN * 16
SLAB = 8
ORDER = (2, 1, 3, 0)
CHUNKS = [(r, e) for r in ORDER for e in (0, 1)]
PANEL = 16
SCHEDULE = (
    "C0", "S0", "C1", "S1", "T0", "T1", "C2", "S2", "C3", "S3", "M0", "P1", "P0", "M1", "C4", "S4",
    "T2", "T4", "M2", "P2", "C5", "S5", "P3", "C6", "F1", "M3", "F0", "P4", "M4", "C7", "S7", "T5",
    "M5", "P5", "S6", "T6", "T3", "F2", "F4", "M7", "P7", "M6", "F3", "P6", "T7", "F5", "F6", "Z0",
    "F7", "Z1",
)
STAGE2 = BF16


def reduce_kernel(
    act_in, grads_in, omega, rows_out, gram_out,
    act, grads, act2, act_t, other, sk, ext, slab, send1, recv1, send2, recv2,
    send3, recv3, send4, recv4, send6, recv9, send8, recv8, send9, recv10, mine,
    part2, recv5, rolled,
    gram, recv6, part, recv7, full, ssem, rsem, lsem,
):
    layers, _, frames, height, width, channels = act_in.shape
    rank = omega.shape[1]
    dp, space = lax.axis_index("dp"), lax.axis_index("space")
    y, core = dp // 2, dp % 2
    x, z = space // RING, space % RING
    other_dp = y * 2 + 1 - core

    def along(axis, step):
        if axis == "x":
            return {"dp": dp, "space": (x + step) % RING * RING + z}
        if axis == "z":
            return {"dp": dp, "space": x * RING + (z + step) % RING}
        return {"dp": (y + step) % RING * 2 + core, "space": space}

    partner = {"dp": other_dp, "space": space}
    spaces = RING * RING
    below, above = (space + 1) % spaces, (space + spaces - 1) % spaces
    turns = [(a, b) for a in range(RING) for b in range(RING) if a or b]
    plane = [
        {"dp": dp, "space": (x + a) % RING * RING + (z + b) % RING} for a, b in turns
    ]
    stack = [along("y", j) for j in (1, 2, 3)]
    crossed = [{"dp": other_dp, "space": below}, {"dp": other_dp, "space": above}]
    peers = [partner] + crossed + plane + stack

    barrier = pltpu.get_barrier_semaphore()
    for peer in peers:
        pl.semaphore_signal(barrier, inc=1, device_id=peer, device_id_type=MESH)

    loads = [
        pltpu.make_async_copy(grads_in.at[1 - core], grads.at[0], lsem.at[0]),
        pltpu.make_async_copy(grads_in.at[core], grads.at[1], lsem.at[1]),
        pltpu.make_async_copy(act_in.at[core], act, lsem.at[2]),
    ]
    for copy in loads:
        copy.start()

    def sketch(n, h):
        flat = grads[n, 0, :, h].reshape(frames * width, channels)
        value = jnp.dot(flat, omega[...], preferred_element_type=F32).astype(BF16)
        return value.reshape(frames, width, rank)

    loads[0].wait()
    for h in range(height):
        other[h] = sketch(0, h)
    loads[1].wait()
    for h in range(height):
        sk[0, 1 + h] = sketch(1, h)

    pl.semaphore_wait(barrier, len(peers))
    sent = []

    def send(src, dst, to):
        at = len(sent)
        copy = pltpu.make_async_remote_copy(
            src_ref=src, dst_ref=dst, send_sem=ssem.at[at], recv_sem=rsem.at[at],
            device_id=to, device_id_type=MESH,
        )
        copy.start()
        sent.append(copy)
        return copy

    halo_copies = [
        [
            send(sk.at[0, height], sk.at[0, 0], {"dp": dp, "space": below}),
            send(sk.at[0, 1], sk.at[0, height + 1], {"dp": dp, "space": above}),
        ],
        [
            send(other.at[height - 1], sk.at[1, 0], crossed[0]),
            send(other.at[0], sk.at[1, height + 1], crossed[1]),
        ],
    ]
    row_copy = send(other, sk.at[1, 1:1 + height], partner)
    act_copy = send(act_in.at[1 - core], act2, partner)

    def transpose(slot, source):
        for h in range(height):
            flat = source[0, :, h].reshape(frames * width, channels)
            at = (slot * height + h) * frames * width
            act_t[:, at:at + frames * width] = flat.T

    column = lax.broadcasted_iota(jnp.int32, (frames * width, rank), 0) % width

    def extend(slot, h):
        value = sk[slot, h].reshape(frames * width, rank).astype(F32)
        if h == 0:
            value = jnp.where(space > 0, value, 0.0)
        if h == height + 1:
            value = jnp.where(space < spaces - 1, value, 0.0)
        ahead = jnp.where(column < width - 1, pltpu.roll(value, frames * width - 1, 0), 0.0)
        behind = jnp.where(column > 0, pltpu.roll(value, 1, 0), 0.0)
        for c, shifted in enumerate((ahead, value, behind)):
            zero = jnp.zeros((width, rank), BF16)
            ext[c, slot, h, 0] = zero
            ext[c, slot, h, frames + 1] = zero
            ext[c, slot, h, 1:1 + frames] = shifted.astype(BF16).reshape(frames, width, rank)

    inner, outer = range(1, 1 + height), (0, height + 1)
    loads[2].wait()
    transpose(0, act)
    for h in inner:
        extend(0, h)
    row_copy.wait_recv()
    for h in inner:
        extend(1, h)
    act_copy.wait_recv()
    transpose(1, act2)
    for slot in range(2):
        for copy, h in zip(halo_copies[slot], outer):
            copy.wait_recv()
            extend(slot, h)

    depth = 2 * height * frames * width

    def compute(r, pairs):
        first = 27 * ((y + r) % RING * 2) // 8

        def columns(k):
            k = jnp.minimum(first + k, 26)
            a, b, c = k // 9, k // 3 % 3, k % 3
            return ext[c, :, pl.ds(2 - b, height), pl.ds(2 - a, frames)].reshape(depth, rank)

        def pair(i, _):
            both = jnp.concatenate([columns(2 * i), columns(2 * i + 1)], axis=1)
            for m in range(3):
                rows = channels // 3
                value = jnp.dot(act_t[m * rows:(m + 1) * rows], both, preferred_element_type=F32)
                for s in range(2):
                    at = pl.multiple_of((2 * i + s) * channels + m * rows, rows)
                    slab[r, pl.ds(at, rows)] = value[:, s * rank:(s + 1) * rank]
            return 0

        lax.fori_loop(pairs[0], pairs[1], pair, 0)

    def window(r, e, mine, o):
        owner = (y + r) % RING * 2 + e
        place = mine * RING + o if e == 0 else o * RING + mine
        start = 27 * owner - 27 * (owner - e) // 8 * 8
        at = start * (channels // 8) + OWN * place // 16 * 16
        return slab[r, pl.ds(pl.multiple_of(at, 16), WIN)]

    first_axis = ("x", "z")
    last_axis = ("z", "x")
    first_at = (x, z)
    last_at = (z, x)
    half = RING // 2
    step1, step2, step3, step4, step5 = {}, {}, {}, {}, {}
    turn1, turn2, turn3 = {}, {}, {}

    def add(pieces):
        return functools.reduce(lambda a, b: a + b.astype(F32), pieces)

    def start1(n):
        r, e = CHUNKS[n]
        cut = 1 + n // 2 % 2
        for o in range(1, RING):
            send1[n, o - 1] = window(r, e, (first_at[e] + 2) % RING, o).astype(BF16)
        step1[n] = [
            send(send1.at[n, :cut], recv1.at[n, :cut], along(first_axis[e], 1)),
            send(send1.at[n, cut:], recv1.at[n, cut:], along(first_axis[e], 3)),
        ]

    def start2(n, s):
        r, e = CHUNKS[n]
        cut = 1 + n // 2 % 2
        step = 1 + 2 * s
        step1[n][s].wait_recv()
        for o in range(1, RING):
            value = window(r, e, (first_at[e] + step) % RING, o)
            if (o <= cut) == (s == 0):
                value = add([value, recv1[n, o - 1]])
            send2[n, s, o - 1] = value.astype(BF16)
        step2.setdefault(n, []).append(
            send(send2.at[n, s], recv2.at[n, s], along(first_axis[e], step))
        )

    def finish1(n):
        r, e = CHUNKS[n]
        cut = 1 + e
        for copy in step2[n]:
            copy.wait_recv()
        if r in (1, 3):
            step3[e][0 if r == 1 else 1].wait_recv()
        if r == 0:
            for copy in step4[e]:
                copy.wait_recv()
        for o in range(1, RING):
            p = o - 1
            value = add([window(r, e, first_at[e], o), recv2[n, 0, p], recv2[n, 1, p]])
            if r == 2:
                send3[e, p] = value.astype(STAGE2)
            elif r == 0:
                part2[e, o] = add([value, recv4[e, 0, p], recv4[e, 1, p]])
            else:
                s = 0 if r == 1 else 1
                if (o <= cut) == (s == 0):
                    value = add([value, recv3[e, p]])
                send4[e, s, p] = value.astype(STAGE2)
        if r == 2:
            step3[e] = [
                send(send3.at[e, :cut], recv3.at[e, :cut], along("y", 1)),
                send(send3.at[e, cut:], recv3.at[e, cut:], along("y", 3)),
            ]
        elif r in (1, 3):
            s = 0 if r == 1 else 1
            step4.setdefault(e, []).append(send(send4.at[e, s], recv4.at[e, s], along("y", r)))

    def turn(n):
        r, e = CHUNKS[n]
        s = 0 if r == 1 else 1
        if r in (1, 3):
            turn1[e][s].wait_recv()
        if r == 0:
            for copy in turn2[e]:
                copy.wait_recv()
        for a in range(RING):
            value = window(r, e, a, 0)
            if r == 2:
                send6[e, a] = value.astype(BF16)
            elif r == 0:
                value = add([value, recv8[e, 0, a], recv8[e, 1, a]])
                send9[e, a] = value.astype(STAGE2)
                mine[e, a] = value
            else:
                if (a < half) == (s == 0):
                    value = add([value, recv9[e, a]])
                send8[e, s, a] = value.astype(BF16)
        if r == 2:
            turn1[e] = [
                send(send6.at[e, :half], recv9.at[e, :half], along("y", 1)),
                send(send6.at[e, half:], recv9.at[e, half:], along("y", 3)),
            ]
        elif r == 0:
            turn3[e] = [
                send(send9.at[e, (first_at[e] + j) % RING], recv10.at[e, j - 1], along(first_axis[e], j))
                for j in (1, 2, 3)
            ]
        else:
            turn2.setdefault(e, []).append(send(send8.at[e, s], recv8.at[e, s], along("y", r)))

    def finish2(e):
        for copy in turn3[e]:
            copy.wait_recv()
        part2[e, 0] = add([mine[e, first_at[e]], recv10[e, 0], recv10[e, 1], recv10[e, 2]])
        step5[e] = [
            send(part2.at[e, (last_at[e] + j) % RING], recv5.at[e, j - 1], along(last_axis[e], j))
            for j in (1, 2, 3)
        ]

    for entry in SCHEDULE:
        n = int(entry[1:])
        if entry[0] == "C":
            r, e = CHUNKS[n]
            compute(r, ((0, 3), (3, 4))[e])
        elif entry[0] in "PM":
            start2(n, "PM".index(entry[0]))
        else:
            {"S": start1, "T": turn, "F": finish1, "Z": finish2}[entry[0]](n)

    shift = 2 * space % 16
    row = lax.broadcasted_iota(jnp.int32, (WIN, rank), 0)
    product = jnp.zeros((rank, rank), F32)
    for e in range(2):
        for copy in step5[e]:
            copy.wait_recv()
        value = part2[e, last_at[e]] + recv5[e, 0] + recv5[e, 1] + recv5[e, 2]
        value = pltpu.roll(value, (WIN - shift) % WIN, 0)
        value = jnp.where(row < OWN, value, 0.0)
        rolled[e] = value
        product = product + lax.dot_general(
            value, value, (((0,), (0,)), ((), ())), precision=HIGHEST, preferred_element_type=F32
        )
    gram[...] = product.reshape(spaces, rank // spaces, rank)

    copies = [send(gram.at[to["space"]], recv6.at[n], to) for n, to in enumerate(plane)]
    rows_copy = send(rolled.at[1 - core], rows_out.at[core], partner)
    rows_out[core] = rolled[core]
    value = gram[space]
    for n, copy in enumerate(copies):
        copy.wait_recv()
        value = value + recv6[n]
    part[0] = value
    copies = [send(part.at[0], recv7.at[n], to) for n, to in enumerate(stack)]
    for n, copy in enumerate(copies):
        copy.wait_recv()
        value = value + recv7[n]
    part[1] = value
    full[space] = value
    copies = [send(part.at[1], full.at[space], to) for to in plane]
    for copy in copies:
        copy.wait_recv()
    copy = send(full, gram_out.at[core], partner)
    gram_out[core] = full[...]
    copy.wait_recv()
    rows_copy.wait_recv()
    for copy in sent:
        copy.wait_send()


def factor_kernel(rows, gram, out, work, inverse, *, scale):
    layers, rank, _ = gram.shape
    lane = lax.broadcasted_iota(jnp.int32, (PANEL, rank), 1)
    row = lax.broadcasted_iota(jnp.int32, (PANEL, rank), 0)
    wide = lax.broadcasted_iota(jnp.int32, (rank, rank), 1)
    work[...] = gram[...]
    for p in range(rank // PANEL):
        first = p * PANEL
        rest = first + PANEL
        at = lane - first
        for l in range(layers):
            lower = work[l, first:rest]
            solved = lower
            cols = [
                jnp.broadcast_to(lower[:, first + j:first + j + 1], (PANEL, rank)) for j in range(PANEL)
            ]
            roots = jnp.ones((PANEL, rank), F32)
            for j in range(PANEL):
                own = row == j
                pivot = jnp.broadcast_to(cols[j][j:j + 1], (PANEL, rank))
                roots = jnp.where(own, pivot, roots)
                scaled = 1.0 / pivot
                mult = cols[j] * scaled
                for i in range(j + 1, PANEL):
                    line = jnp.broadcast_to(cols[i][j:j + 1], (PANEL, rank))
                    cols[i] = jnp.where(own, line * scaled, cols[i] - mult * line)
                line = jnp.broadcast_to(solved[j:j + 1], (PANEL, rank))
                pick = jnp.where(own, scaled, -mult)
                solved = jnp.where(at == j, pick, jnp.where(own, line * scaled, solved - mult * line))
                below = jnp.where(row > j, mult, 0.0)
                updated = lower - below * lower[j:j + 1]
                lower = jnp.where((at == j) & (row > j), -mult, updated)
            lower = jnp.where(at < row, lower, jnp.where(at == row, 1.0, 0.0))
            inverse[l, first:rest] = lower / jnp.sqrt(roots)
            if rest < rank:
                parts = [jnp.zeros((first, rank), F32)] if first else []
                parts += [solved, jnp.zeros((rank - rest, rank), F32)]
                left = work[l, rest:]
                step = jnp.dot(
                    left, jnp.concatenate(parts, axis=0), precision=HIGHEST, preferred_element_type=F32
                )
                inside = (wide[rest:] >= first) & (wide[rest:] < rest)
                work[l, rest:] = jnp.where(inside, 0.0, left) - step
    for l in range(layers):
        value = lax.dot_general(
            rows[l], inverse[l], (((1,), (1,)), ((), ())),
            precision=HIGHEST, preferred_element_type=F32,
        )
        out[:, l] = (value * scale)[:OWN]


def shards(activations, out_grads, omega):
    layers, clips, frames, height, width, channels = activations.shape
    rank = omega.shape[1]
    chunks = len(CHUNKS)
    vmem = pl.BlockSpec(memory_space=pltpu.VMEM)
    blocks, fewer = (RING, WIN, rank), (RING - 1, WIN, rank)
    gram_blocks = (RING * RING, rank // (RING * RING), rank)
    rows, gram = pl.pallas_call(
        reduce_kernel,
        name="reduce",
        out_shape=(
            jax.ShapeDtypeStruct((layers, WIN, rank), F32),
            jax.ShapeDtypeStruct((layers,) + gram_blocks, F32),
        ),
        in_specs=[pl.BlockSpec(memory_space=pl.ANY)] * 2 + [vmem],
        out_specs=(vmem, vmem),
        scratch_shapes=[
            pltpu.VMEM(activations.shape[1:], BF16),
            pltpu.VMEM(activations.shape, BF16),
            pltpu.VMEM(activations.shape[1:], BF16),
            pltpu.VMEM((channels, 2 * height * frames * width), BF16),
            pltpu.VMEM((height, frames, width, rank), BF16),
            pltpu.VMEM((2, height + 2, frames, width, rank), BF16),
            pltpu.VMEM((3, 2, height + 2, frames + 2, width, rank), BF16),
            pltpu.VMEM((RING, SLAB * channels, rank), F32),
            pltpu.VMEM((chunks,) + fewer, BF16),
            pltpu.VMEM((chunks,) + fewer, BF16),
            pltpu.VMEM((chunks, 2) + fewer, BF16),
            pltpu.VMEM((chunks, 2) + fewer, BF16),
            pltpu.VMEM((2,) + fewer, STAGE2),
            pltpu.VMEM((2,) + fewer, STAGE2),
            pltpu.VMEM((2, 2) + fewer, STAGE2),
            pltpu.VMEM((2, 2) + fewer, STAGE2),
            pltpu.VMEM((2,) + blocks, BF16),
            pltpu.VMEM((2,) + blocks, BF16),
            pltpu.VMEM((2, 2) + blocks, BF16),
            pltpu.VMEM((2, 2) + blocks, BF16),
            pltpu.VMEM((2,) + blocks, STAGE2),
            pltpu.VMEM((2,) + fewer, STAGE2),
            pltpu.VMEM((2,) + blocks, F32),
            pltpu.VMEM((2,) + blocks, F32),
            pltpu.VMEM((2, 3, WIN, rank), F32),
            pltpu.VMEM((2, WIN, rank), F32),
            pltpu.VMEM(gram_blocks, F32),
            pltpu.VMEM((RING * RING - 1,) + gram_blocks[1:], F32),
            pltpu.VMEM((2,) + gram_blocks[1:], F32),
            pltpu.VMEM((RING - 1,) + gram_blocks[1:], F32),
            pltpu.VMEM(gram_blocks, F32),
            pltpu.SemaphoreType.DMA((112,)),
            pltpu.SemaphoreType.DMA((112,)),
            pltpu.SemaphoreType.DMA((3,)),
        ],
        compiler_params=pltpu.CompilerParams(
            collective_id=0, has_side_effects=True, vmem_limit_bytes=60 * 2**20
        ),
    )(activations, out_grads, omega)
    basis = pl.pallas_call(
        functools.partial(factor_kernel, scale=math.sqrt(27 * channels)),
        name="factor",
        out_shape=jax.ShapeDtypeStruct((OWN, layers, rank), F32),
        in_specs=[vmem] * 2,
        out_specs=vmem,
        scratch_shapes=[
            pltpu.VMEM((layers, rank, rank), F32),
            pltpu.VMEM((layers, rank, rank), F32),
        ],
    )(rows, gram.reshape(layers, rank, rank))
    return jnp.transpose(basis, (1, 0, 2))


def solution(mesh):
    return jax.shard_map(
        shards,
        mesh=mesh,
        in_specs=(
            P(None, "dp", None, "space", None, None),
            P(None, "dp", None, "space", None, None),
            P(),
        ),
        out_specs=P(None, ("dp", "space"), None),
        check_vma=False,
    )
```

```python
import functools
import math

import jax
import jax.numpy as jnp
from jax import lax
from jax.experimental import pallas as pl
from jax.experimental.pallas import tpu as pltpu
from jax.sharding import PartitionSpec as P

MESH = pl.DeviceIdType.MESH
BF16, F32 = jnp.bfloat16, jnp.float32
HIGHEST = lax.Precision.HIGHEST
RING = 4
OWN = 162
WIN = 176
BLOCK = OWN * 16
SLAB = 8
ORDER = (2, 1, 3, 0)
CHUNKS = [(r, e) for r in ORDER for e in (0, 1)]
PANEL = 16
SCHEDULE = (
    "C0", "S0", "C1", "S1", "T0", "T1", "C2", "S2", "C3", "S3", "M0", "P1", "P0", "M1", "C4", "S4",
    "T2", "T4", "M2", "P2", "C5", "S5", "P3", "C6", "F1", "M3", "F0", "P4", "M4", "C7", "S7", "T5",
    "M5", "P5", "S6", "T6", "T3", "F2", "F4", "M7", "P7", "M6", "F3", "P6", "T7", "F5", "F6", "Z0",
    "F7", "Z1",
)
STAGE2 = BF16


def factor(work, inverse):
    rank = work.shape[0]
    lane = lax.broadcasted_iota(jnp.int32, (PANEL, rank), 1)
    row = lax.broadcasted_iota(jnp.int32, (PANEL, rank), 0)
    wide = lax.broadcasted_iota(jnp.int32, (rank, rank), 1)
    for p in range(rank // PANEL):
        first = p * PANEL
        rest = first + PANEL
        at = lane - first
        lower = work[first:rest]
        solved = lower
        cols = [
            jnp.broadcast_to(lower[:, first + j:first + j + 1], (PANEL, rank)) for j in range(PANEL)
        ]
        roots = jnp.ones((PANEL, rank), F32)
        for j in range(PANEL):
            own = row == j
            pivot = jnp.broadcast_to(cols[j][j:j + 1], (PANEL, rank))
            roots = jnp.where(own, pivot, roots)
            scaled = 1.0 / pivot
            mult = cols[j] * scaled
            for i in range(j + 1, PANEL):
                line = jnp.broadcast_to(cols[i][j:j + 1], (PANEL, rank))
                cols[i] = jnp.where(own, line * scaled, cols[i] - mult * line)
            line = jnp.broadcast_to(solved[j:j + 1], (PANEL, rank))
            pick = jnp.where(own, scaled, -mult)
            solved = jnp.where(at == j, pick, jnp.where(own, line * scaled, solved - mult * line))
            below = jnp.where(row > j, mult, 0.0)
            updated = lower - below * lower[j:j + 1]
            lower = jnp.where((at == j) & (row > j), -mult, updated)
        lower = jnp.where(at < row, lower, jnp.where(at == row, 1.0, 0.0))
        inverse[first:rest] = lower / jnp.sqrt(roots)
        if rest < rank:
            parts = [jnp.zeros((first, rank), F32)] if first else []
            parts += [solved, jnp.zeros((rank - rest, rank), F32)]
            left = work[rest:]
            step = jnp.dot(
                left, jnp.concatenate(parts, axis=0), precision=HIGHEST, preferred_element_type=F32
            )
            inside = (wide[rest:] >= first) & (wide[rest:] < rest)
            work[rest:] = jnp.where(inside, 0.0, left) - step


def reduce_kernel(
    act_in, grads_in, omega_in, out,
    omega, act, grads, act2, act_t, other, sk, ext, slab, send1, recv1, send2, recv2,
    send3, recv3, send4, recv4, send6, recv9, send8, recv8, send9, recv10, mine,
    part2, recv5, rolled,
    gram, recv6, part, recv7, full, rows_in, work, inverse, inverse_in, ssem, rsem, lsem, *, scale,
):
    layers, _, frames, height, width, channels = act_in.shape
    rank = omega_in.shape[1]
    dp, space = lax.axis_index("dp"), lax.axis_index("space")
    y, core = dp // 2, dp % 2
    x, z = space // RING, space % RING
    other_dp = y * 2 + 1 - core

    def along(axis, step):
        if axis == "x":
            return {"dp": dp, "space": (x + step) % RING * RING + z}
        if axis == "z":
            return {"dp": dp, "space": x * RING + (z + step) % RING}
        return {"dp": (y + step) % RING * 2 + core, "space": space}

    partner = {"dp": other_dp, "space": space}
    spaces = RING * RING
    below, above = (space + 1) % spaces, (space + spaces - 1) % spaces
    turns = [(a, b) for a in range(RING) for b in range(RING) if a or b]
    plane = [
        {"dp": dp, "space": (x + a) % RING * RING + (z + b) % RING} for a, b in turns
    ]
    stack = [along("y", j) for j in (1, 2, 3)]
    crossed = [{"dp": other_dp, "space": below}, {"dp": other_dp, "space": above}]
    peers = [partner] + crossed + plane + stack

    barrier = pltpu.get_barrier_semaphore()
    for peer in peers:
        pl.semaphore_signal(barrier, inc=1, device_id=peer, device_id_type=MESH)

    loads = [
        pltpu.make_async_copy(grads_in.at[1 - core], grads.at[0], lsem.at[0]),
        pltpu.make_async_copy(grads_in.at[core], grads.at[1], lsem.at[1]),
        pltpu.make_async_copy(act_in.at[core], act, lsem.at[2]),
        pltpu.make_async_copy(omega_in, omega, lsem.at[3]),
    ]
    for n in (3, 0, 1, 2):
        loads[n].start()

    def sketch(n, h):
        flat = grads[n, 0, :, h].reshape(frames * width, channels)
        value = jnp.dot(flat, omega[...], preferred_element_type=F32).astype(BF16)
        return value.reshape(frames, width, rank)

    loads[3].wait()
    loads[0].wait()
    for h in range(height):
        other[h] = sketch(0, h)
    loads[1].wait()
    for h in range(height):
        sk[0, 1 + h] = sketch(1, h)

    pl.semaphore_wait(barrier, len(peers))
    sent = []

    def send(src, dst, to):
        at = len(sent)
        copy = pltpu.make_async_remote_copy(
            src_ref=src, dst_ref=dst, send_sem=ssem.at[at], recv_sem=rsem.at[at],
            device_id=to, device_id_type=MESH,
        )
        copy.start()
        sent.append(copy)
        return copy

    halo_copies = [
        [
            send(sk.at[0, height], sk.at[0, 0], {"dp": dp, "space": below}),
            send(sk.at[0, 1], sk.at[0, height + 1], {"dp": dp, "space": above}),
        ],
        [
            send(other.at[height - 1], sk.at[1, 0], crossed[0]),
            send(other.at[0], sk.at[1, height + 1], crossed[1]),
        ],
    ]
    row_copy = send(other, sk.at[1, 1:1 + height], partner)
    act_copy = send(act_in.at[1 - core], act2, partner)

    def transpose(slot, source):
        for h in range(height):
            flat = source[0, :, h].reshape(frames * width, channels)
            at = (slot * height + h) * frames * width
            act_t[:, at:at + frames * width] = flat.T

    column = lax.broadcasted_iota(jnp.int32, (frames * width, rank), 0) % width

    def extend(slot, h):
        value = sk[slot, h].reshape(frames * width, rank).astype(F32)
        if h == 0:
            value = jnp.where(space > 0, value, 0.0)
        if h == height + 1:
            value = jnp.where(space < spaces - 1, value, 0.0)
        ahead = jnp.where(column < width - 1, pltpu.roll(value, frames * width - 1, 0), 0.0)
        behind = jnp.where(column > 0, pltpu.roll(value, 1, 0), 0.0)
        for c, shifted in enumerate((ahead, value, behind)):
            zero = jnp.zeros((width, rank), BF16)
            ext[c, slot, h, 0] = zero
            ext[c, slot, h, frames + 1] = zero
            ext[c, slot, h, 1:1 + frames] = shifted.astype(BF16).reshape(frames, width, rank)

    inner, outer = range(1, 1 + height), (0, height + 1)
    loads[2].wait()
    transpose(0, act)
    for h in inner:
        extend(0, h)
    row_copy.wait_recv()
    for h in inner:
        extend(1, h)
    act_copy.wait_recv()
    transpose(1, act2)
    for slot in range(2):
        for copy, h in zip(halo_copies[slot], outer):
            copy.wait_recv()
            extend(slot, h)

    depth = 2 * height * frames * width

    def compute(r, pairs):
        first = 27 * ((y + r) % RING * 2) // 8

        def columns(k):
            k = jnp.minimum(first + k, 26)
            a, b, c = k // 9, k // 3 % 3, k % 3
            return ext[c, :, pl.ds(2 - b, height), pl.ds(2 - a, frames)].reshape(depth, rank)

        def pair(i, _):
            both = jnp.concatenate([columns(2 * i), columns(2 * i + 1)], axis=1)
            for m in range(3):
                rows = channels // 3
                value = jnp.dot(act_t[m * rows:(m + 1) * rows], both, preferred_element_type=F32)
                for s in range(2):
                    at = pl.multiple_of((2 * i + s) * channels + m * rows, rows)
                    slab[r, pl.ds(at, rows)] = value[:, s * rank:(s + 1) * rank]
            return 0

        lax.fori_loop(pairs[0], pairs[1], pair, 0)

    def window(r, e, mine, o):
        owner = (y + r) % RING * 2 + e
        place = mine * RING + o if e == 0 else o * RING + mine
        start = 27 * owner - 27 * (owner - e) // 8 * 8
        at = start * (channels // 8) + OWN * place // 16 * 16
        return slab[r, pl.ds(pl.multiple_of(at, 16), WIN)]

    first_axis = ("x", "z")
    last_axis = ("z", "x")
    first_at = (x, z)
    last_at = (z, x)
    half = RING // 2
    step1, step2, step3, step4, step5 = {}, {}, {}, {}, {}
    turn1, turn2, turn3 = {}, {}, {}

    def add(pieces):
        return functools.reduce(lambda a, b: a + b.astype(F32), pieces)

    def start1(n):
        r, e = CHUNKS[n]
        cut = 1 + n // 2 % 2
        for o in range(1, RING):
            send1[n, o - 1] = window(r, e, (first_at[e] + 2) % RING, o).astype(BF16)
        step1[n] = [
            send(send1.at[n, :cut], recv1.at[n, :cut], along(first_axis[e], 1)),
            send(send1.at[n, cut:], recv1.at[n, cut:], along(first_axis[e], 3)),
        ]

    def start2(n, s):
        r, e = CHUNKS[n]
        cut = 1 + n // 2 % 2
        step = 1 + 2 * s
        step1[n][s].wait_recv()
        for o in range(1, RING):
            value = window(r, e, (first_at[e] + step) % RING, o)
            if (o <= cut) == (s == 0):
                value = add([value, recv1[n, o - 1]])
            send2[n, s, o - 1] = value.astype(BF16)
        step2.setdefault(n, []).append(
            send(send2.at[n, s], recv2.at[n, s], along(first_axis[e], step))
        )

    def finish1(n):
        r, e = CHUNKS[n]
        cut = 1 + e
        for copy in step2[n]:
            copy.wait_recv()
        if r in (1, 3):
            step3[e][0 if r == 1 else 1].wait_recv()
        if r == 0:
            for copy in step4[e]:
                copy.wait_recv()
        for o in range(1, RING):
            p = o - 1
            value = add([window(r, e, first_at[e], o), recv2[n, 0, p], recv2[n, 1, p]])
            if r == 2:
                send3[e, p] = value.astype(STAGE2)
            elif r == 0:
                part2[e, o] = add([value, recv4[e, 0, p], recv4[e, 1, p]])
            else:
                s = 0 if r == 1 else 1
                if (o <= cut) == (s == 0):
                    value = add([value, recv3[e, p]])
                send4[e, s, p] = value.astype(STAGE2)
        if r == 2:
            step3[e] = [
                send(send3.at[e, :cut], recv3.at[e, :cut], along("y", 1)),
                send(send3.at[e, cut:], recv3.at[e, cut:], along("y", 3)),
            ]
        elif r in (1, 3):
            s = 0 if r == 1 else 1
            step4.setdefault(e, []).append(send(send4.at[e, s], recv4.at[e, s], along("y", r)))

    def turn(n):
        r, e = CHUNKS[n]
        s = 0 if r == 1 else 1
        if r in (1, 3):
            turn1[e][s].wait_recv()
        if r == 0:
            for copy in turn2[e]:
                copy.wait_recv()
        for a in range(RING):
            value = window(r, e, a, 0)
            if r == 2:
                send6[e, a] = value.astype(BF16)
            elif r == 0:
                value = add([value, recv8[e, 0, a], recv8[e, 1, a]])
                send9[e, a] = value.astype(STAGE2)
                mine[e, a] = value
            else:
                if (a < half) == (s == 0):
                    value = add([value, recv9[e, a]])
                send8[e, s, a] = value.astype(BF16)
        if r == 2:
            turn1[e] = [
                send(send6.at[e, :half], recv9.at[e, :half], along("y", 1)),
                send(send6.at[e, half:], recv9.at[e, half:], along("y", 3)),
            ]
        elif r == 0:
            turn3[e] = [
                send(send9.at[e, (first_at[e] + j) % RING], recv10.at[e, j - 1], along(first_axis[e], j))
                for j in (1, 2, 3)
            ]
        else:
            turn2.setdefault(e, []).append(send(send8.at[e, s], recv8.at[e, s], along("y", r)))

    def finish2(e):
        for copy in turn3[e]:
            copy.wait_recv()
        part2[e, 0] = add([mine[e, first_at[e]], recv10[e, 0], recv10[e, 1], recv10[e, 2]])
        step5[e] = [
            send(part2.at[e, (last_at[e] + j) % RING], recv5.at[e, j - 1], along(last_axis[e], j))
            for j in (1, 2, 3)
        ]

    for entry in SCHEDULE:
        n = int(entry[1:])
        if entry[0] == "C":
            r, e = CHUNKS[n]
            compute(r, ((0, 3), (3, 4))[e])
        elif entry[0] in "PM":
            start2(n, "PM".index(entry[0]))
        else:
            {"S": start1, "T": turn, "F": finish1, "Z": finish2}[entry[0]](n)

    shift = 2 * space % 16
    row = lax.broadcasted_iota(jnp.int32, (WIN, rank), 0)
    product = jnp.zeros((rank, rank), F32)
    for e in range(2):
        for copy in step5[e]:
            copy.wait_recv()
        value = part2[e, last_at[e]] + recv5[e, 0] + recv5[e, 1] + recv5[e, 2]
        value = pltpu.roll(value, (WIN - shift) % WIN, 0)
        value = jnp.where(row < OWN, value, 0.0)
        rolled[e] = value
        product = product + lax.dot_general(
            value, value, (((0,), (0,)), ((), ())), precision=HIGHEST, preferred_element_type=F32
        )
    gram[...] = product.reshape(spaces, rank // spaces, rank)

    copies = [send(gram.at[to["space"]], recv6.at[n], to) for n, to in enumerate(plane)]
    rows_copy = send(rolled.at[1 - core], rows_in, partner)
    value = gram[space]
    for n, copy in enumerate(copies):
        copy.wait_recv()
        value = value + recv6[n]
    part[0] = value
    copies = [send(part.at[0], recv7.at[n], to) for n, to in enumerate(stack)]
    for n, copy in enumerate(copies):
        copy.wait_recv()
        value = value + recv7[n]
    part[1] = value
    full[space] = value
    copies = [send(part.at[1], full.at[space], to) for to in plane]
    for copy in copies:
        copy.wait_recv()

    work[...] = full[...].reshape(rank, rank)
    factor(work, inverse)
    copy = send(inverse, inverse_in, partner)

    def solve(rows, lower):
        value = lax.dot_general(
            rows, lower, (((1,), (1,)), ((), ())), precision=HIGHEST, preferred_element_type=F32
        )
        return (value * scale)[:OWN]

    near = solve(rolled[core], inverse[...])
    rows_copy.wait_recv()
    copy.wait_recv()
    far = solve(rows_in[...], inverse_in[...])
    out[:, 0] = jnp.where(core == 0, near, far)
    out[:, 1] = jnp.where(core == 0, far, near)
    for copy in sent:
        copy.wait_send()


def shards(activations, out_grads, omega):
    layers, clips, frames, height, width, channels = activations.shape
    rank = omega.shape[1]
    chunks = len(CHUNKS)
    vmem = pl.BlockSpec(memory_space=pltpu.VMEM)
    blocks, fewer = (RING, WIN, rank), (RING - 1, WIN, rank)
    gram_blocks = (RING * RING, rank // (RING * RING), rank)
    basis = pl.pallas_call(
        functools.partial(reduce_kernel, scale=math.sqrt(27 * channels)),
        name="refresh",
        out_shape=jax.ShapeDtypeStruct((OWN, layers, rank), F32),
        in_specs=[pl.BlockSpec(memory_space=pltpu.HBM)] * 3,
        out_specs=vmem,
        scratch_shapes=[
            pltpu.VMEM(omega.shape, BF16),
            pltpu.VMEM(activations.shape[1:], BF16),
            pltpu.VMEM(activations.shape, BF16),
            pltpu.VMEM(activations.shape[1:], BF16),
            pltpu.VMEM((channels, 2 * height * frames * width), BF16),
            pltpu.VMEM((height, frames, width, rank), BF16),
            pltpu.VMEM((2, height + 2, frames, width, rank), BF16),
            pltpu.VMEM((3, 2, height + 2, frames + 2, width, rank), BF16),
            pltpu.VMEM((RING, SLAB * channels, rank), F32),
            pltpu.VMEM((chunks,) + fewer, BF16),
            pltpu.VMEM((chunks,) + fewer, BF16),
            pltpu.VMEM((chunks, 2) + fewer, BF16),
            pltpu.VMEM((chunks, 2) + fewer, BF16),
            pltpu.VMEM((2,) + fewer, STAGE2),
            pltpu.VMEM((2,) + fewer, STAGE2),
            pltpu.VMEM((2, 2) + fewer, STAGE2),
            pltpu.VMEM((2, 2) + fewer, STAGE2),
            pltpu.VMEM((2,) + blocks, BF16),
            pltpu.VMEM((2,) + blocks, BF16),
            pltpu.VMEM((2, 2) + blocks, BF16),
            pltpu.VMEM((2, 2) + blocks, BF16),
            pltpu.VMEM((2,) + blocks, STAGE2),
            pltpu.VMEM((2,) + fewer, STAGE2),
            pltpu.VMEM((2,) + blocks, F32),
            pltpu.VMEM((2,) + blocks, F32),
            pltpu.VMEM((2, 3, WIN, rank), F32),
            pltpu.VMEM((2, WIN, rank), F32),
            pltpu.VMEM(gram_blocks, F32),
            pltpu.VMEM((RING * RING - 1,) + gram_blocks[1:], F32),
            pltpu.VMEM((2,) + gram_blocks[1:], F32),
            pltpu.VMEM((RING - 1,) + gram_blocks[1:], F32),
            pltpu.VMEM(gram_blocks, F32),
            pltpu.VMEM((WIN, rank), F32),
            pltpu.VMEM((rank, rank), F32),
            pltpu.VMEM((rank, rank), F32),
            pltpu.VMEM((rank, rank), F32),
            pltpu.SemaphoreType.DMA((112,)),
            pltpu.SemaphoreType.DMA((112,)),
            pltpu.SemaphoreType.DMA((4,)),
        ],
        compiler_params=pltpu.CompilerParams(
            collective_id=0, has_side_effects=True, vmem_limit_bytes=13721 * 4096
        ),
    )(activations, out_grads, omega)
    return jnp.transpose(basis, (1, 0, 2))


def solution(mesh):
    return jax.shard_map(
        shards,
        mesh=mesh,
        in_specs=(
            P(None, "dp", None, "space", None, None),
            P(None, "dp", None, "space", None, None),
            P(),
        ),
        out_specs=P(None, ("dp", "space"), None),
        check_vma=False,
    )
```

```python
import functools
import math

import jax
import jax.numpy as jnp
from jax import lax
from jax.experimental import pallas as pl
from jax.experimental.pallas import tpu as pltpu
from jax.sharding import PartitionSpec as P

MESH = pl.DeviceIdType.MESH
BF16, F32 = jnp.bfloat16, jnp.float32
HIGHEST = lax.Precision.HIGHEST
RING = 4
OWN = 162
WIN = 176
BLOCK = OWN * 16
SLAB = 8
ORDER = (2, 1, 3, 0)
CHUNKS = [(r, e) for r in ORDER for e in (0, 1)]
PANEL = 16
EARLY = ORDER
SCHEDULE = (
    "C0", "S0", "C1", "S1", "T0", "T1", "C2", "S2", "C3", "S3", "M0", "P1", "P0", "M1", "C4", "S4",
    "T2", "T4", "M2", "P2", "C5", "S5", "P3", "C6", "F1", "M3", "F0", "P4", "M4", "C7", "S7", "T5",
    "M5", "P5", "S6", "T6", "T3", "F2", "F4", "M7", "P7", "M6", "F3", "P6", "T7", "F5", "F6", "Z0",
    "F7", "Z1",
)
STAGE2 = BF16


def factor(work, inverse):
    rank = work.shape[0]
    lane = lax.broadcasted_iota(jnp.int32, (PANEL, rank), 1)
    row = lax.broadcasted_iota(jnp.int32, (PANEL, rank), 0)
    wide = lax.broadcasted_iota(jnp.int32, (rank, rank), 1)
    for p in range(rank // PANEL):
        first = p * PANEL
        rest = first + PANEL
        at = lane - first
        lower = work[first:rest]
        solved = lower
        cols = [
            jnp.broadcast_to(lower[:, first + j:first + j + 1], (PANEL, rank)) for j in range(PANEL)
        ]
        roots = jnp.ones((PANEL, rank), F32)
        for j in range(PANEL):
            own = row == j
            pivot = jnp.broadcast_to(cols[j][j:j + 1], (PANEL, rank))
            roots = jnp.where(own, pivot, roots)
            scaled = 1.0 / pivot
            mult = cols[j] * scaled
            for i in range(j + 1, PANEL):
                line = jnp.broadcast_to(cols[i][j:j + 1], (PANEL, rank))
                cols[i] = jnp.where(own, line * scaled, cols[i] - mult * line)
            line = jnp.broadcast_to(solved[j:j + 1], (PANEL, rank))
            pick = jnp.where(own, scaled, -mult)
            solved = jnp.where(at == j, pick, jnp.where(own, line * scaled, solved - mult * line))
            below = jnp.where(row > j, mult, 0.0)
            updated = lower - below * lower[j:j + 1]
            lower = jnp.where((at == j) & (row > j), -mult, updated)
        lower = jnp.where(at < row, lower, jnp.where(at == row, 1.0, 0.0))
        inverse[first:rest] = lower / jnp.sqrt(roots)
        if rest < rank:
            parts = [jnp.zeros((first, rank), F32)] if first else []
            parts += [solved, jnp.zeros((rank - rest, rank), F32)]
            left = work[rest:]
            step = jnp.dot(
                left, jnp.concatenate(parts, axis=0), precision=HIGHEST, preferred_element_type=F32
            )
            inside = (wide[rest:] >= first) & (wide[rest:] < rest)
            work[rest:] = jnp.where(inside, 0.0, left) - step


def reduce_kernel(
    act_in, grads_in, omega_in, out,
    omega, act, grads, act2, act_t, other, sk, ext, slab, send1, recv1, send2, recv2,
    send3, recv3, send4, recv4, send6, recv9, send8, recv8, send9, recv10, mine,
    part2, recv5, rolled,
    gram, recv6, part, recv7, full, rows_in, work, inverse, inverse_in, ssem, rsem, lsem, *, scale,
):
    layers, _, frames, height, width, channels = act_in.shape
    rank = omega_in.shape[1]
    dp, space = lax.axis_index("dp"), lax.axis_index("space")
    y, core = dp // 2, dp % 2
    x, z = space // RING, space % RING
    other_dp = y * 2 + 1 - core

    def along(axis, step):
        if axis == "x":
            return {"dp": dp, "space": (x + step) % RING * RING + z}
        if axis == "z":
            return {"dp": dp, "space": x * RING + (z + step) % RING}
        return {"dp": (y + step) % RING * 2 + core, "space": space}

    partner = {"dp": other_dp, "space": space}
    spaces = RING * RING
    below, above = (space + 1) % spaces, (space + spaces - 1) % spaces
    turns = [(a, b) for a in range(RING) for b in range(RING) if a or b]
    plane = [
        {"dp": dp, "space": (x + a) % RING * RING + (z + b) % RING} for a, b in turns
    ]
    stack = [along("y", j) for j in (1, 2, 3)]
    crossed = [{"dp": other_dp, "space": below}, {"dp": other_dp, "space": above}]
    peers = [partner] + crossed + plane + stack

    barrier = pltpu.get_barrier_semaphore()
    for peer in peers:
        pl.semaphore_signal(barrier, inc=1, device_id=peer, device_id_type=MESH)

    loads = [
        pltpu.make_async_copy(grads_in.at[1 - core], grads.at[0], lsem.at[0]),
        pltpu.make_async_copy(grads_in.at[core], grads.at[1], lsem.at[1]),
        pltpu.make_async_copy(act_in.at[core], act, lsem.at[2]),
        pltpu.make_async_copy(omega_in, omega, lsem.at[3]),
    ]
    for n in (3, 0, 1, 2):
        loads[n].start()

    def sketch(n, h):
        flat = grads[n, 0, :, h].reshape(frames * width, channels)
        value = jnp.dot(flat, omega[...], preferred_element_type=F32).astype(BF16)
        return value.reshape(frames, width, rank)

    loads[3].wait()
    loads[0].wait()
    for h in range(height):
        other[h] = sketch(0, h)
    loads[1].wait()
    for h in range(height):
        sk[0, 1 + h] = sketch(1, h)

    pl.semaphore_wait(barrier, len(peers))
    sent = []

    def send(src, dst, to):
        at = len(sent)
        copy = pltpu.make_async_remote_copy(
            src_ref=src, dst_ref=dst, send_sem=ssem.at[at], recv_sem=rsem.at[at],
            device_id=to, device_id_type=MESH,
        )
        copy.start()
        sent.append(copy)
        return copy

    halo_copies = [
        [
            send(sk.at[0, height], sk.at[0, 0], {"dp": dp, "space": below}),
            send(sk.at[0, 1], sk.at[0, height + 1], {"dp": dp, "space": above}),
        ],
        [
            send(other.at[height - 1], sk.at[1, 0], crossed[0]),
            send(other.at[0], sk.at[1, height + 1], crossed[1]),
        ],
    ]
    row_copy = send(other, sk.at[1, 1:1 + height], partner)
    act_copy = send(act_in.at[1 - core], act2, partner)

    def transpose(slot, source):
        for h in range(height):
            flat = source[0, :, h].reshape(frames * width, channels)
            at = (slot * height + h) * frames * width
            act_t[:, at:at + frames * width] = flat.T

    column = lax.broadcasted_iota(jnp.int32, (frames * width, rank), 0) % width

    def extend(slot, h):
        value = sk[slot, h].reshape(frames * width, rank).astype(F32)
        if h == 0:
            value = jnp.where(space > 0, value, 0.0)
        if h == height + 1:
            value = jnp.where(space < spaces - 1, value, 0.0)
        ahead = jnp.where(column < width - 1, pltpu.roll(value, frames * width - 1, 0), 0.0)
        behind = jnp.where(column > 0, pltpu.roll(value, 1, 0), 0.0)
        for c, shifted in enumerate((ahead, value, behind)):
            zero = jnp.zeros((width, rank), BF16)
            ext[c, slot, h, 0] = zero
            ext[c, slot, h, frames + 1] = zero
            ext[c, slot, h, 1:1 + frames] = shifted.astype(BF16).reshape(frames, width, rank)

    inner, outer = range(1, 1 + height), (0, height + 1)
    loads[2].wait()
    transpose(0, act)
    for h in inner:
        extend(0, h)
    row_copy.wait_recv()
    for h in inner:
        extend(1, h)
    act_copy.wait_recv()
    transpose(1, act2)
    depth = 2 * height * frames * width

    def compute(r, pairs):
        first = 27 * ((y + r) % RING * 2) // 8

        def columns(k):
            k = jnp.minimum(first + k, 26)
            a, b, c = k // 9, k // 3 % 3, k % 3
            return ext[c, :, pl.ds(2 - b, height), pl.ds(2 - a, frames)].reshape(depth, rank)

        early = (y + r + 2) % RING if r in EARLY else SLAB

        def pair(i):
            both = jnp.concatenate([columns(2 * i), columns(2 * i + 1)], axis=1)
            for m in range(3):
                rows = channels // 3
                value = jnp.dot(act_t[m * rows:(m + 1) * rows], both, preferred_element_type=F32)
                for s in range(2):
                    at = pl.multiple_of((2 * i + s) * channels + m * rows, rows)
                    slab[r, pl.ds(at, rows)] = value[:, s * rank:(s + 1) * rank]

        def step(i, _):
            @pl.when(i != early)
            def _():
                pair(i)

            return 0

        if pairs is None:
            pair(early)
        else:
            lax.fori_loop(pairs[0], pairs[1], step, 0)

    for r in EARLY:
        compute(r, None)

    for slot in range(2):
        for copy, h in zip(halo_copies[slot], outer):
            copy.wait_recv()
            extend(slot, h)

    def window(r, e, mine, o):
        owner = (y + r) % RING * 2 + e
        place = mine * RING + o if e == 0 else o * RING + mine
        start = 27 * owner - 27 * (owner - e) // 8 * 8
        at = start * (channels // 8) + OWN * place // 16 * 16
        return slab[r, pl.ds(pl.multiple_of(at, 16), WIN)]

    first_axis = ("x", "z")
    last_axis = ("z", "x")
    first_at = (x, z)
    last_at = (z, x)
    half = RING // 2
    step1, step2, step3, step4, step5 = {}, {}, {}, {}, {}
    turn1, turn2, turn3 = {}, {}, {}

    def add(pieces):
        return functools.reduce(lambda a, b: a + b.astype(F32), pieces)

    def start1(n):
        r, e = CHUNKS[n]
        cut = 1 + n // 2 % 2
        for o in range(1, RING):
            send1[n, o - 1] = window(r, e, (first_at[e] + 2) % RING, o).astype(BF16)
        step1[n] = [
            send(send1.at[n, :cut], recv1.at[n, :cut], along(first_axis[e], 1)),
            send(send1.at[n, cut:], recv1.at[n, cut:], along(first_axis[e], 3)),
        ]

    def start2(n, s):
        r, e = CHUNKS[n]
        cut = 1 + n // 2 % 2
        step = 1 + 2 * s
        step1[n][s].wait_recv()
        for o in range(1, RING):
            value = window(r, e, (first_at[e] + step) % RING, o)
            if (o <= cut) == (s == 0):
                value = add([value, recv1[n, o - 1]])
            send2[n, s, o - 1] = value.astype(BF16)
        step2.setdefault(n, []).append(
            send(send2.at[n, s], recv2.at[n, s], along(first_axis[e], step))
        )

    def finish1(n):
        r, e = CHUNKS[n]
        cut = 1 + e
        for copy in step2[n]:
            copy.wait_recv()
        if r in (1, 3):
            step3[e][0 if r == 1 else 1].wait_recv()
        if r == 0:
            for copy in step4[e]:
                copy.wait_recv()
        for o in range(1, RING):
            p = o - 1
            value = add([window(r, e, first_at[e], o), recv2[n, 0, p], recv2[n, 1, p]])
            if r == 2:
                send3[e, p] = value.astype(STAGE2)
            elif r == 0:
                part2[e, o] = add([value, recv4[e, 0, p], recv4[e, 1, p]])
            else:
                s = 0 if r == 1 else 1
                if (o <= cut) == (s == 0):
                    value = add([value, recv3[e, p]])
                send4[e, s, p] = value.astype(STAGE2)
        if r == 2:
            step3[e] = [
                send(send3.at[e, :cut], recv3.at[e, :cut], along("y", 1)),
                send(send3.at[e, cut:], recv3.at[e, cut:], along("y", 3)),
            ]
        elif r in (1, 3):
            s = 0 if r == 1 else 1
            step4.setdefault(e, []).append(send(send4.at[e, s], recv4.at[e, s], along("y", r)))

    def turn(n):
        r, e = CHUNKS[n]
        s = 0 if r == 1 else 1
        if r in (1, 3):
            turn1[e][s].wait_recv()
        if r == 0:
            for copy in turn2[e]:
                copy.wait_recv()
        for a in range(RING):
            value = window(r, e, a, 0)
            if r == 2:
                send6[e, a] = value.astype(BF16)
            elif r == 0:
                value = add([value, recv8[e, 0, a], recv8[e, 1, a]])
                send9[e, a] = value.astype(STAGE2)
                mine[e, a] = value
            else:
                if (a < half) == (s == 0):
                    value = add([value, recv9[e, a]])
                send8[e, s, a] = value.astype(BF16)
        if r == 2:
            turn1[e] = [
                send(send6.at[e, :half], recv9.at[e, :half], along("y", 1)),
                send(send6.at[e, half:], recv9.at[e, half:], along("y", 3)),
            ]
        elif r == 0:
            turn3[e] = [
                send(send9.at[e, (first_at[e] + j) % RING], recv10.at[e, j - 1], along(first_axis[e], j))
                for j in (1, 2, 3)
            ]
        else:
            turn2.setdefault(e, []).append(send(send8.at[e, s], recv8.at[e, s], along("y", r)))

    def finish2(e):
        for copy in turn3[e]:
            copy.wait_recv()
        part2[e, 0] = add([mine[e, first_at[e]], recv10[e, 0], recv10[e, 1], recv10[e, 2]])
        step5[e] = [
            send(part2.at[e, (last_at[e] + j) % RING], recv5.at[e, j - 1], along(last_axis[e], j))
            for j in (1, 2, 3)
        ]

    for entry in SCHEDULE:
        n = int(entry[1:])
        if entry[0] == "C":
            r, e = CHUNKS[n]
            compute(r, ((0, 3), (3, 4))[e])
        elif entry[0] in "PM":
            start2(n, "PM".index(entry[0]))
        else:
            {"S": start1, "T": turn, "F": finish1, "Z": finish2}[entry[0]](n)

    shift = 2 * space % 16
    row = lax.broadcasted_iota(jnp.int32, (WIN, rank), 0)
    product = jnp.zeros((rank, rank), F32)
    for e in range(2):
        for copy in step5[e]:
            copy.wait_recv()
        value = part2[e, last_at[e]] + recv5[e, 0] + recv5[e, 1] + recv5[e, 2]
        value = pltpu.roll(value, (WIN - shift) % WIN, 0)
        value = jnp.where(row < OWN, value, 0.0)
        rolled[e] = value
        product = product + lax.dot_general(
            value, value, (((0,), (0,)), ((), ())), precision=HIGHEST, preferred_element_type=F32
        )
    gram[...] = product.reshape(spaces, rank // spaces, rank)

    copies = [send(gram.at[to["space"]], recv6.at[n], to) for n, to in enumerate(plane)]
    rows_copy = send(rolled.at[1 - core], rows_in, partner)
    value = gram[space]
    for n, copy in enumerate(copies):
        copy.wait_recv()
        value = value + recv6[n]
    part[0] = value
    copies = [send(part.at[0], recv7.at[n], to) for n, to in enumerate(stack)]
    for n, copy in enumerate(copies):
        copy.wait_recv()
        value = value + recv7[n]
    part[1] = value
    full[space] = value
    copies = [send(part.at[1], full.at[space], to) for to in plane]
    for copy in copies:
        copy.wait_recv()

    work[...] = full[...].reshape(rank, rank)
    factor(work, inverse)
    copy = send(inverse, inverse_in, partner)

    def solve(rows, lower):
        value = lax.dot_general(
            rows, lower, (((1,), (1,)), ((), ())), precision=HIGHEST, preferred_element_type=F32
        )
        return (value * scale)[:OWN]

    near = solve(rolled[core], inverse[...])
    rows_copy.wait_recv()
    copy.wait_recv()
    far = solve(rows_in[...], inverse_in[...])
    out[:, 0] = jnp.where(core == 0, near, far)
    out[:, 1] = jnp.where(core == 0, far, near)
    for copy in sent:
        copy.wait_send()


def shards(activations, out_grads, omega):
    layers, clips, frames, height, width, channels = activations.shape
    rank = omega.shape[1]
    chunks = len(CHUNKS)
    vmem = pl.BlockSpec(memory_space=pltpu.VMEM)
    blocks, fewer = (RING, WIN, rank), (RING - 1, WIN, rank)
    gram_blocks = (RING * RING, rank // (RING * RING), rank)
    basis = pl.pallas_call(
        functools.partial(reduce_kernel, scale=math.sqrt(27 * channels)),
        name="refresh",
        out_shape=jax.ShapeDtypeStruct((OWN, layers, rank), F32),
        in_specs=[pl.BlockSpec(memory_space=pltpu.HBM)] * 3,
        out_specs=vmem,
        scratch_shapes=[
            pltpu.VMEM(omega.shape, BF16),
            pltpu.VMEM(activations.shape[1:], BF16),
            pltpu.VMEM(activations.shape, BF16),
            pltpu.VMEM(activations.shape[1:], BF16),
            pltpu.VMEM((channels, 2 * height * frames * width), BF16),
            pltpu.VMEM((height, frames, width, rank), BF16),
            pltpu.VMEM((2, height + 2, frames, width, rank), BF16),
            pltpu.VMEM((3, 2, height + 2, frames + 2, width, rank), BF16),
            pltpu.VMEM((RING, SLAB * channels, rank), F32),
            pltpu.VMEM((chunks,) + fewer, BF16),
            pltpu.VMEM((chunks,) + fewer, BF16),
            pltpu.VMEM((chunks, 2) + fewer, BF16),
            pltpu.VMEM((chunks, 2) + fewer, BF16),
            pltpu.VMEM((2,) + fewer, STAGE2),
            pltpu.VMEM((2,) + fewer, STAGE2),
            pltpu.VMEM((2, 2) + fewer, STAGE2),
            pltpu.VMEM((2, 2) + fewer, STAGE2),
            pltpu.VMEM((2,) + blocks, BF16),
            pltpu.VMEM((2,) + blocks, BF16),
            pltpu.VMEM((2, 2) + blocks, BF16),
            pltpu.VMEM((2, 2) + blocks, BF16),
            pltpu.VMEM((2,) + blocks, STAGE2),
            pltpu.VMEM((2,) + fewer, STAGE2),
            pltpu.VMEM((2,) + blocks, F32),
            pltpu.VMEM((2,) + blocks, F32),
            pltpu.VMEM((2, 3, WIN, rank), F32),
            pltpu.VMEM((2, WIN, rank), F32),
            pltpu.VMEM(gram_blocks, F32),
            pltpu.VMEM((RING * RING - 1,) + gram_blocks[1:], F32),
            pltpu.VMEM((2,) + gram_blocks[1:], F32),
            pltpu.VMEM((RING - 1,) + gram_blocks[1:], F32),
            pltpu.VMEM(gram_blocks, F32),
            pltpu.VMEM((WIN, rank), F32),
            pltpu.VMEM((rank, rank), F32),
            pltpu.VMEM((rank, rank), F32),
            pltpu.VMEM((rank, rank), F32),
            pltpu.SemaphoreType.DMA((112,)),
            pltpu.SemaphoreType.DMA((112,)),
            pltpu.SemaphoreType.DMA((4,)),
        ],
        compiler_params=pltpu.CompilerParams(
            collective_id=0, has_side_effects=True, vmem_limit_bytes=13721 * 4096
        ),
    )(activations, out_grads, omega)
    return jnp.transpose(basis, (1, 0, 2))


def solution(mesh):
    return jax.shard_map(
        shards,
        mesh=mesh,
        in_specs=(
            P(None, "dp", None, "space", None, None),
            P(None, "dp", None, "space", None, None),
            P(),
        ),
        out_specs=P(None, ("dp", "space"), None),
        check_vma=False,
    )
```

```python
import functools
import math

import jax
import jax.numpy as jnp
from jax import lax
from jax.experimental import pallas as pl
from jax.experimental.pallas import tpu as pltpu
from jax.sharding import PartitionSpec as P

MESH = pl.DeviceIdType.MESH
BF16, F32 = jnp.bfloat16, jnp.float32
HIGHEST = lax.Precision.HIGHEST
RING = 4
OWN = 162
WIN = 176
BLOCK = OWN * 16
SLAB = 8
ORDER = (2, 1, 3, 0)
CHUNKS = [(r, e) for r in ORDER for e in (0, 1)]
PANEL = 16
EARLY = ORDER
SCHEDULE = (
    "C0", "S0", "C1", "S1", "T0", "T1", "C2", "S2", "C3", "S3", "M0", "P1", "P0", "M1", "C4", "S4",
    "T2", "T4", "M2", "P2", "C5", "S5", "P3", "C6", "F1", "M3", "F0", "P4", "M4", "C7", "S7", "T5",
    "M5", "P5", "S6", "T6", "T3", "F2", "F4", "M7", "P7", "M6", "F3", "P6", "T7", "F5", "F6", "Z0",
    "F7", "Z1",
)
STAGE2 = BF16


def factor(work, inverse):
    rank = work.shape[0]
    lane = lax.broadcasted_iota(jnp.int32, (PANEL, rank), 1)
    row = lax.broadcasted_iota(jnp.int32, (PANEL, rank), 0)
    wide = lax.broadcasted_iota(jnp.int32, (rank, rank), 1)
    for p in range(rank // PANEL):
        first = p * PANEL
        rest = first + PANEL
        at = lane - first
        lower = work[first:rest]
        solved = lower
        cols = [
            jnp.broadcast_to(lower[:, first + j:first + j + 1], (PANEL, rank)) for j in range(PANEL)
        ]
        roots = jnp.ones((PANEL, rank), F32)
        for j in range(PANEL):
            own = row == j
            pivot = jnp.broadcast_to(cols[j][j:j + 1], (PANEL, rank))
            roots = jnp.where(own, pivot, roots)
            scaled = 1.0 / pivot
            mult = cols[j] * scaled
            for i in range(j + 1, PANEL):
                line = jnp.broadcast_to(cols[i][j:j + 1], (PANEL, rank))
                cols[i] = jnp.where(own, line * scaled, cols[i] - mult * line)
            line = jnp.broadcast_to(solved[j:j + 1], (PANEL, rank))
            pick = jnp.where(own, scaled, -mult)
            solved = jnp.where(at == j, pick, jnp.where(own, line * scaled, solved - mult * line))
            below = jnp.where(row > j, mult, 0.0)
            updated = lower - below * lower[j:j + 1]
            lower = jnp.where((at == j) & (row > j), -mult, updated)
        lower = jnp.where(at < row, lower, jnp.where(at == row, 1.0, 0.0))
        inverse[first:rest] = lower / jnp.sqrt(roots)
        if rest < rank:
            parts = [jnp.zeros((first, rank), F32)] if first else []
            parts += [solved, jnp.zeros((rank - rest, rank), F32)]
            left = work[rest:]
            step = jnp.dot(
                left, jnp.concatenate(parts, axis=0), precision=HIGHEST, preferred_element_type=F32
            )
            inside = (wide[rest:] >= first) & (wide[rest:] < rest)
            work[rest:] = jnp.where(inside, 0.0, left) - step


def reduce_kernel(
    act_in, grads_in, omega_in, out,
    omega, act, grads, act2, act_t, other, sk, ext, slab, send1, recv1, send2, recv2,
    send3, recv3, send4, recv4, send6, recv9, send8, recv8, send9, recv10, mine,
    part2, recv5, rolled,
    gram, recv6, part, recv7, full, rows_in, work, inverse, inverse_in, ssem, rsem, lsem, *, scale,
):
    layers, _, frames, height, width, channels = act_in.shape
    rank = omega_in.shape[1]
    dp, space = lax.axis_index("dp"), lax.axis_index("space")
    y, core = dp // 2, dp % 2
    x, z = space // RING, space % RING
    other_dp = y * 2 + 1 - core

    def along(axis, step):
        if axis == "x":
            return {"dp": dp, "space": (x + step) % RING * RING + z}
        if axis == "z":
            return {"dp": dp, "space": x * RING + (z + step) % RING}
        return {"dp": (y + step) % RING * 2 + core, "space": space}

    partner = {"dp": other_dp, "space": space}
    spaces = RING * RING
    below, above = (space + 1) % spaces, (space + spaces - 1) % spaces
    turns = [(a, b) for a in range(RING) for b in range(RING) if a or b]
    turns.sort(key=lambda t: -(min(t[0], RING - t[0]) + min(t[1], RING - t[1])))
    plane = [
        {"dp": dp, "space": (x + a) % RING * RING + (z + b) % RING} for a, b in turns
    ]
    stack = [along("y", j) for j in (1, 2, 3)]
    crossed = [{"dp": other_dp, "space": below}, {"dp": other_dp, "space": above}]
    peers = [partner] + crossed + plane + stack

    barrier = pltpu.get_barrier_semaphore()
    for peer in peers:
        pl.semaphore_signal(barrier, inc=1, device_id=peer, device_id_type=MESH)

    loads = [
        pltpu.make_async_copy(grads_in.at[1 - core], grads.at[0], lsem.at[0]),
        pltpu.make_async_copy(grads_in.at[core], grads.at[1], lsem.at[1]),
        pltpu.make_async_copy(act_in.at[core], act, lsem.at[2]),
        pltpu.make_async_copy(omega_in, omega, lsem.at[3]),
    ]
    for n in (3, 0, 1, 2):
        loads[n].start()

    def sketch(n, h):
        flat = grads[n, 0, :, h].reshape(frames * width, channels)
        value = jnp.dot(flat, omega[...], preferred_element_type=F32).astype(BF16)
        return value.reshape(frames, width, rank)

    loads[3].wait()
    loads[0].wait()
    for h in range(height):
        other[h] = sketch(0, h)
    loads[1].wait()
    for h in range(height):
        sk[0, 1 + h] = sketch(1, h)

    pl.semaphore_wait(barrier, len(peers))
    sent = []

    def send(src, dst, to):
        at = len(sent)
        copy = pltpu.make_async_remote_copy(
            src_ref=src, dst_ref=dst, send_sem=ssem.at[at], recv_sem=rsem.at[at],
            device_id=to, device_id_type=MESH,
        )
        copy.start()
        sent.append(copy)
        return copy

    def settle(last):
        while settled[0] < last:
            sent[settled[0]].wait_send()
            settled[0] += 1

    settled = [0]
    halo_copies = [
        [
            send(sk.at[0, height], sk.at[0, 0], {"dp": dp, "space": below}),
            send(sk.at[0, 1], sk.at[0, height + 1], {"dp": dp, "space": above}),
        ],
        [
            send(other.at[height - 1], sk.at[1, 0], crossed[0]),
            send(other.at[0], sk.at[1, height + 1], crossed[1]),
        ],
    ]
    row_copy = send(other, sk.at[1, 1:1 + height], partner)
    act_copy = send(act_in.at[1 - core], act2, partner)

    def transpose(slot, source):
        for h in range(height):
            flat = source[0, :, h].reshape(frames * width, channels)
            at = (slot * height + h) * frames * width
            act_t[:, at:at + frames * width] = flat.T

    column = lax.broadcasted_iota(jnp.int32, (frames * width, rank), 0) % width

    def extend(slot, h):
        value = sk[slot, h].reshape(frames * width, rank).astype(F32)
        if h == 0:
            value = jnp.where(space > 0, value, 0.0)
        if h == height + 1:
            value = jnp.where(space < spaces - 1, value, 0.0)
        ahead = jnp.where(column < width - 1, pltpu.roll(value, frames * width - 1, 0), 0.0)
        behind = jnp.where(column > 0, pltpu.roll(value, 1, 0), 0.0)
        for c, shifted in enumerate((ahead, value, behind)):
            zero = jnp.zeros((width, rank), BF16)
            ext[c, slot, h, 0] = zero
            ext[c, slot, h, frames + 1] = zero
            ext[c, slot, h, 1:1 + frames] = shifted.astype(BF16).reshape(frames, width, rank)

    inner, outer = range(1, 1 + height), (0, height + 1)
    loads[2].wait()
    transpose(0, act)
    for h in inner:
        extend(0, h)
    row_copy.wait_recv()
    for h in inner:
        extend(1, h)
    act_copy.wait_recv()
    transpose(1, act2)
    depth = 2 * height * frames * width

    def compute(r, pairs):
        first = 27 * ((y + r) % RING * 2) // 8

        def columns(k):
            k = jnp.minimum(first + k, 26)
            a, b, c = k // 9, k // 3 % 3, k % 3
            return ext[c, :, pl.ds(2 - b, height), pl.ds(2 - a, frames)].reshape(depth, rank)

        early = (y + r + 2) % RING if r in EARLY else SLAB

        def pair(i):
            both = jnp.concatenate([columns(2 * i), columns(2 * i + 1)], axis=1)
            for m in range(3):
                rows = channels // 3
                value = jnp.dot(act_t[m * rows:(m + 1) * rows], both, preferred_element_type=F32)
                for s in range(2):
                    at = pl.multiple_of((2 * i + s) * channels + m * rows, rows)
                    slab[r, pl.ds(at, rows)] = value[:, s * rank:(s + 1) * rank]

        def step(i, _):
            @pl.when(i != early)
            def _():
                pair(i)

            return 0

        if pairs is None:
            pair(early)
        else:
            lax.fori_loop(pairs[0], pairs[1], step, 0)

    for r in EARLY:
        compute(r, None)

    for slot in range(2):
        for copy, h in zip(halo_copies[slot], outer):
            copy.wait_recv()
            extend(slot, h)

    def window(r, e, mine, o):
        owner = (y + r) % RING * 2 + e
        place = mine * RING + o if e == 0 else o * RING + mine
        start = 27 * owner - 27 * (owner - e) // 8 * 8
        at = start * (channels // 8) + OWN * place // 16 * 16
        return slab[r, pl.ds(pl.multiple_of(at, 16), WIN)]

    first_axis = ("x", "z")
    last_axis = ("z", "x")
    first_at = (x, z)
    last_at = (z, x)
    half = RING // 2
    step1, step2, step3, step4, step5 = {}, {}, {}, {}, {}
    turn1, turn2, turn3 = {}, {}, {}

    def add(pieces):
        return functools.reduce(lambda a, b: a + b.astype(F32), pieces)

    def start1(n):
        r, e = CHUNKS[n]
        cut = 1 + n // 2 % 2
        for o in range(1, RING):
            send1[n, o - 1] = window(r, e, (first_at[e] + 2) % RING, o).astype(BF16)
        step1[n] = [
            send(send1.at[n, :cut], recv1.at[n, :cut], along(first_axis[e], 1)),
            send(send1.at[n, cut:], recv1.at[n, cut:], along(first_axis[e], 3)),
        ]

    def start2(n, s):
        r, e = CHUNKS[n]
        cut = 1 + n // 2 % 2
        step = 1 + 2 * s
        step1[n][s].wait_recv()
        for o in range(1, RING):
            value = window(r, e, (first_at[e] + step) % RING, o)
            if (o <= cut) == (s == 0):
                value = add([value, recv1[n, o - 1]])
            send2[n, s, o - 1] = value.astype(BF16)
        step2.setdefault(n, []).append(
            send(send2.at[n, s], recv2.at[n, s], along(first_axis[e], step))
        )

    def finish1(n):
        r, e = CHUNKS[n]
        cut = 1 + e
        for copy in step2[n]:
            copy.wait_recv()
        if r in (1, 3):
            step3[e][0 if r == 1 else 1].wait_recv()
        if r == 0:
            for copy in step4[e]:
                copy.wait_recv()
        for o in range(1, RING):
            p = o - 1
            value = add([window(r, e, first_at[e], o), recv2[n, 0, p], recv2[n, 1, p]])
            if r == 2:
                send3[e, p] = value.astype(STAGE2)
            elif r == 0:
                part2[e, o] = add([value, recv4[e, 0, p], recv4[e, 1, p]])
            else:
                s = 0 if r == 1 else 1
                if (o <= cut) == (s == 0):
                    value = add([value, recv3[e, p]])
                send4[e, s, p] = value.astype(STAGE2)
        if r == 2:
            step3[e] = [
                send(send3.at[e, :cut], recv3.at[e, :cut], along("y", 1)),
                send(send3.at[e, cut:], recv3.at[e, cut:], along("y", 3)),
            ]
        elif r in (1, 3):
            s = 0 if r == 1 else 1
            step4.setdefault(e, []).append(send(send4.at[e, s], recv4.at[e, s], along("y", r)))

    def turn(n):
        r, e = CHUNKS[n]
        s = 0 if r == 1 else 1
        if r in (1, 3):
            turn1[e][s].wait_recv()
        if r == 0:
            for copy in turn2[e]:
                copy.wait_recv()
        for a in range(RING):
            value = window(r, e, a, 0)
            if r == 2:
                send6[e, a] = value.astype(BF16)
            elif r == 0:
                value = add([value, recv8[e, 0, a], recv8[e, 1, a]])
                send9[e, a] = value.astype(STAGE2)
                mine[e, a] = value
            else:
                if (a < half) == (s == 0):
                    value = add([value, recv9[e, a]])
                send8[e, s, a] = value.astype(BF16)
        if r == 2:
            turn1[e] = [
                send(send6.at[e, :half], recv9.at[e, :half], along("y", 1)),
                send(send6.at[e, half:], recv9.at[e, half:], along("y", 3)),
            ]
        elif r == 0:
            turn3[e] = [
                send(send9.at[e, (first_at[e] + j) % RING], recv10.at[e, j - 1], along(first_axis[e], j))
                for j in (1, 2, 3)
            ]
        else:
            turn2.setdefault(e, []).append(send(send8.at[e, s], recv8.at[e, s], along("y", r)))

    def finish2(e):
        for copy in turn3[e]:
            copy.wait_recv()
        part2[e, 0] = add([mine[e, first_at[e]], recv10[e, 0], recv10[e, 1], recv10[e, 2]])
        step5[e] = [
            send(part2.at[e, (last_at[e] + j) % RING], recv5.at[e, j - 1], along(last_axis[e], j))
            for j in (1, 2, 3)
        ]

    for entry in SCHEDULE:
        n = int(entry[1:])
        if entry[0] == "C":
            r, e = CHUNKS[n]
            compute(r, ((0, 3), (3, 4))[e])
        elif entry[0] in "PM":
            start2(n, "PM".index(entry[0]))
        else:
            {"S": start1, "T": turn, "F": finish1, "Z": finish2}[entry[0]](n)

    shift = 2 * space % 16
    row = lax.broadcasted_iota(jnp.int32, (WIN, rank), 0)
    product = jnp.zeros((rank, rank), F32)
    for e in range(2):
        for copy in step5[e]:
            copy.wait_recv()
        value = part2[e, last_at[e]] + recv5[e, 0] + recv5[e, 1] + recv5[e, 2]
        value = pltpu.roll(value, (WIN - shift) % WIN, 0)
        value = jnp.where(row < OWN, value, 0.0)
        rolled[e] = value
        product = product + lax.dot_general(
            value, value, (((0,), (0,)), ((), ())), precision=HIGHEST, preferred_element_type=F32
        )
    gram[...] = product.reshape(spaces, rank // spaces, rank)

    copies = [send(gram.at[to["space"]], recv6.at[n], to) for n, to in enumerate(plane)]
    rows_copy = send(rolled.at[1 - core], rows_in, partner)
    settle(len(sent) - len(copies) - 1)
    value = gram[space]
    for n, copy in reversed(list(enumerate(copies))):
        copy.wait_recv()
        value = value + recv6[n]
    part[0] = value
    copies = [send(part.at[0], recv7.at[n], to) for n, to in enumerate(stack)]
    settle(len(sent) - len(copies))
    for n, copy in enumerate(copies):
        copy.wait_recv()
        value = value + recv7[n]
    part[1] = value
    full[space] = value
    copies = [send(part.at[1], full.at[space], to) for to in plane]
    settle(len(sent) - len(copies))
    for copy in copies:
        copy.wait_recv()

    work[...] = full[...].reshape(rank, rank)
    factor(work, inverse)
    copy = send(inverse, inverse_in, partner)
    settle(len(sent) - 1)

    def solve(rows, lower):
        value = lax.dot_general(
            rows, lower, (((1,), (1,)), ((), ())), precision=HIGHEST, preferred_element_type=F32
        )
        return (value * scale)[:OWN]

    near = solve(rolled[core], inverse[...])
    rows_copy.wait_recv()
    copy.wait_recv()
    far = solve(rows_in[...], inverse_in[...])
    out[:, 0] = jnp.where(core == 0, near, far)
    out[:, 1] = jnp.where(core == 0, far, near)
    settle(len(sent))


def shards(activations, out_grads, omega):
    layers, clips, frames, height, width, channels = activations.shape
    rank = omega.shape[1]
    chunks = len(CHUNKS)
    vmem = pl.BlockSpec(memory_space=pltpu.VMEM)
    blocks, fewer = (RING, WIN, rank), (RING - 1, WIN, rank)
    gram_blocks = (RING * RING, rank // (RING * RING), rank)
    basis = pl.pallas_call(
        functools.partial(reduce_kernel, scale=math.sqrt(27 * channels)),
        name="refresh",
        out_shape=jax.ShapeDtypeStruct((OWN, layers, rank), F32),
        in_specs=[pl.BlockSpec(memory_space=pltpu.HBM)] * 3,
        out_specs=vmem,
        scratch_shapes=[
            pltpu.VMEM(omega.shape, BF16),
            pltpu.VMEM(activations.shape[1:], BF16),
            pltpu.VMEM(activations.shape, BF16),
            pltpu.VMEM(activations.shape[1:], BF16),
            pltpu.VMEM((channels, 2 * height * frames * width), BF16),
            pltpu.VMEM((height, frames, width, rank), BF16),
            pltpu.VMEM((2, height + 2, frames, width, rank), BF16),
            pltpu.VMEM((3, 2, height + 2, frames + 2, width, rank), BF16),
            pltpu.VMEM((RING, SLAB * channels, rank), F32),
            pltpu.VMEM((chunks,) + fewer, BF16),
            pltpu.VMEM((chunks,) + fewer, BF16),
            pltpu.VMEM((chunks, 2) + fewer, BF16),
            pltpu.VMEM((chunks, 2) + fewer, BF16),
            pltpu.VMEM((2,) + fewer, STAGE2),
            pltpu.VMEM((2,) + fewer, STAGE2),
            pltpu.VMEM((2, 2) + fewer, STAGE2),
            pltpu.VMEM((2, 2) + fewer, STAGE2),
            pltpu.VMEM((2,) + blocks, BF16),
            pltpu.VMEM((2,) + blocks, BF16),
            pltpu.VMEM((2, 2) + blocks, BF16),
            pltpu.VMEM((2, 2) + blocks, BF16),
            pltpu.VMEM((2,) + blocks, STAGE2),
            pltpu.VMEM((2,) + fewer, STAGE2),
            pltpu.VMEM((2,) + blocks, F32),
            pltpu.VMEM((2,) + blocks, F32),
            pltpu.VMEM((2, 3, WIN, rank), F32),
            pltpu.VMEM((2, WIN, rank), F32),
            pltpu.VMEM(gram_blocks, F32),
            pltpu.VMEM((RING * RING - 1,) + gram_blocks[1:], F32),
            pltpu.VMEM((2,) + gram_blocks[1:], F32),
            pltpu.VMEM((RING - 1,) + gram_blocks[1:], F32),
            pltpu.VMEM(gram_blocks, F32),
            pltpu.VMEM((WIN, rank), F32),
            pltpu.VMEM((rank, rank), F32),
            pltpu.VMEM((rank, rank), F32),
            pltpu.VMEM((rank, rank), F32),
            pltpu.SemaphoreType.DMA((112,)),
            pltpu.SemaphoreType.DMA((112,)),
            pltpu.SemaphoreType.DMA((4,)),
        ],
        compiler_params=pltpu.CompilerParams(
            collective_id=0, has_side_effects=True, vmem_limit_bytes=13721 * 4096
        ),
    )(activations, out_grads, omega)
    return jnp.transpose(basis, (1, 0, 2))


def solution(mesh):
    return jax.shard_map(
        shards,
        mesh=mesh,
        in_specs=(
            P(None, "dp", None, "space", None, None),
            P(None, "dp", None, "space", None, None),
            P(),
        ),
        out_specs=P(None, ("dp", "space"), None),
        check_vma=False,
    )
```

```python
import functools
import math

import jax
import jax.numpy as jnp
from jax import lax
from jax.experimental import pallas as pl
from jax.experimental.pallas import tpu as pltpu
from jax.sharding import PartitionSpec as P

MESH = pl.DeviceIdType.MESH
BF16, F32 = jnp.bfloat16, jnp.float32
HIGHEST = lax.Precision.HIGHEST
RING = 4
OWN = 162
WIN = 176
BLOCK = OWN * 16
SLAB = 8
ORDER = (2, 1, 3, 0)
CHUNKS = [(r, e) for r in ORDER for e in (0, 1)]
PANEL = 16
EARLY = ORDER
SCHEDULE = (
    "C0", "S0", "C1", "S1", "T0", "T1", "C2", "S2", "C3", "S3", "M0", "P1", "P0", "M1", "C4", "S4",
    "T2", "T4", "M2", "P2", "C5", "S5", "P3", "C6", "F1", "M3", "F0", "P4", "M4", "C7", "S7", "T5",
    "M5", "P5", "S6", "T6", "T3", "F2", "F4", "M7", "P7", "M6", "F3", "P6", "T7", "F5", "F6", "Z0",
    "F7", "Z1",
)
STAGE2 = BF16


def factor(work, inverse):
    rank = work.shape[0]
    lane = lax.broadcasted_iota(jnp.int32, (PANEL, rank), 1)
    row = lax.broadcasted_iota(jnp.int32, (PANEL, rank), 0)
    wide = lax.broadcasted_iota(jnp.int32, (rank, rank), 1)
    for p in range(rank // PANEL):
        first = p * PANEL
        rest = first + PANEL
        at = lane - first
        lower = work[first:rest]
        solved = lower
        cols = [
            jnp.broadcast_to(lower[:, first + j:first + j + 1], (PANEL, rank)) for j in range(PANEL)
        ]
        roots = jnp.ones((PANEL, rank), F32)
        for j in range(PANEL):
            own = row == j
            pivot = jnp.broadcast_to(cols[j][j:j + 1], (PANEL, rank))
            roots = jnp.where(own, pivot, roots)
            scaled = 1.0 / pivot
            mult = cols[j] * scaled
            for i in range(j + 1, PANEL):
                line = jnp.broadcast_to(cols[i][j:j + 1], (PANEL, rank))
                cols[i] = jnp.where(own, line * scaled, cols[i] - mult * line)
            line = jnp.broadcast_to(solved[j:j + 1], (PANEL, rank))
            pick = jnp.where(own, scaled, -mult)
            solved = jnp.where(at == j, pick, jnp.where(own, line * scaled, solved - mult * line))
            below = jnp.where(row > j, mult, 0.0)
            updated = lower - below * lower[j:j + 1]
            lower = jnp.where((at == j) & (row > j), -mult, updated)
        lower = jnp.where(at < row, lower, jnp.where(at == row, 1.0, 0.0))
        inverse[first:rest] = lower / jnp.sqrt(roots)
        if rest < rank:
            parts = [jnp.zeros((first, rank), F32)] if first else []
            parts += [solved, jnp.zeros((rank - rest, rank), F32)]
            left = work[rest:]
            step = jnp.dot(
                left, jnp.concatenate(parts, axis=0), precision=HIGHEST, preferred_element_type=F32
            )
            inside = (wide[rest:] >= first) & (wide[rest:] < rest)
            work[rest:] = jnp.where(inside, 0.0, left) - step


def reduce_kernel(
    act_in, grads_in, omega_in, out,
    omega, act, grads, act2, act_t, other, sk, ext, slab, send1, recv1, send2, recv2,
    send3, recv3, send4, recv4, send6, recv9, send8, recv8, send9, recv10, mine,
    part2, recv5, rolled,
    gram, recv6, part, recv7, full, rows_in, work, inverse, inverse_in, ssem, rsem, lsem, *, scale,
):
    layers, _, frames, height, width, channels = act_in.shape
    rank = omega_in.shape[1]
    dp, space = lax.axis_index("dp"), lax.axis_index("space")
    y, core = dp // 2, dp % 2
    x, z = space // RING, space % RING
    other_dp = y * 2 + 1 - core

    def along(axis, step):
        if axis == "x":
            return {"dp": dp, "space": (x + step) % RING * RING + z}
        if axis == "z":
            return {"dp": dp, "space": x * RING + (z + step) % RING}
        return {"dp": (y + step) % RING * 2 + core, "space": space}

    partner = {"dp": other_dp, "space": space}
    spaces = RING * RING
    below, above = (space + 1) % spaces, (space + spaces - 1) % spaces
    turns = [(a, b) for a in range(RING) for b in range(RING) if a or b]
    turns.sort(key=lambda t: -(min(t[0], RING - t[0]) + min(t[1], RING - t[1])))
    plane = [
        {"dp": dp, "space": (x + a) % RING * RING + (z + b) % RING} for a, b in turns
    ]
    stack = [along("y", j) for j in (2, 1, 3)]
    crossed = [{"dp": other_dp, "space": below}, {"dp": other_dp, "space": above}]
    peers = [partner] + crossed + plane + stack

    barrier = pltpu.get_barrier_semaphore()
    for peer in peers:
        pl.semaphore_signal(barrier, inc=1, device_id=peer, device_id_type=MESH)

    loads = [
        pltpu.make_async_copy(grads_in.at[1 - core], grads.at[0], lsem.at[0]),
        pltpu.make_async_copy(grads_in.at[core], grads.at[1], lsem.at[1]),
        pltpu.make_async_copy(act_in.at[core], act, lsem.at[2]),
        pltpu.make_async_copy(omega_in, omega, lsem.at[3]),
    ]
    for n in (3, 0, 1, 2):
        loads[n].start()

    def sketch(n, h):
        flat = grads[n, 0, :, h].reshape(frames * width, channels)
        value = jnp.dot(flat, omega[...], preferred_element_type=F32).astype(BF16)
        return value.reshape(frames, width, rank)

    loads[3].wait()
    loads[0].wait()
    for h in range(height):
        other[h] = sketch(0, h)
    loads[1].wait()
    for h in range(height):
        sk[0, 1 + h] = sketch(1, h)

    pl.semaphore_wait(barrier, len(peers))
    sent = []

    def send(src, dst, to):
        at = len(sent)
        copy = pltpu.make_async_remote_copy(
            src_ref=src, dst_ref=dst, send_sem=ssem.at[at], recv_sem=rsem.at[at],
            device_id=to, device_id_type=MESH,
        )
        copy.start()
        sent.append(copy)
        return copy

    def settle(last):
        while settled[0] < last:
            sent[settled[0]].wait_send()
            settled[0] += 1

    settled = [0]
    halo_copies = [
        [
            send(sk.at[0, height], sk.at[0, 0], {"dp": dp, "space": below}),
            send(sk.at[0, 1], sk.at[0, height + 1], {"dp": dp, "space": above}),
        ],
        [
            send(other.at[height - 1], sk.at[1, 0], crossed[0]),
            send(other.at[0], sk.at[1, height + 1], crossed[1]),
        ],
    ]
    row_copy = send(other, sk.at[1, 1:1 + height], partner)
    act_copy = send(act_in.at[1 - core], act2, partner)

    def transpose(slot, source):
        for h in range(height):
            flat = source[0, :, h].reshape(frames * width, channels)
            at = (slot * height + h) * frames * width
            act_t[:, at:at + frames * width] = flat.T

    column = lax.broadcasted_iota(jnp.int32, (frames * width, rank), 0) % width

    def extend(slot, h):
        value = sk[slot, h].reshape(frames * width, rank).astype(F32)
        if h == 0:
            value = jnp.where(space > 0, value, 0.0)
        if h == height + 1:
            value = jnp.where(space < spaces - 1, value, 0.0)
        ahead = jnp.where(column < width - 1, pltpu.roll(value, frames * width - 1, 0), 0.0)
        behind = jnp.where(column > 0, pltpu.roll(value, 1, 0), 0.0)
        for c, shifted in enumerate((ahead, value, behind)):
            zero = jnp.zeros((width, rank), BF16)
            ext[c, slot, h, 0] = zero
            ext[c, slot, h, frames + 1] = zero
            ext[c, slot, h, 1:1 + frames] = shifted.astype(BF16).reshape(frames, width, rank)

    inner, outer = range(1, 1 + height), (0, height + 1)
    loads[2].wait()
    transpose(0, act)
    for h in inner:
        extend(0, h)
    row_copy.wait_recv()
    for h in inner:
        extend(1, h)
    act_copy.wait_recv()
    transpose(1, act2)
    depth = 2 * height * frames * width

    def compute(r, pairs):
        first = 27 * ((y + r) % RING * 2) // 8

        def columns(k):
            k = jnp.minimum(first + k, 26)
            a, b, c = k // 9, k // 3 % 3, k % 3
            return ext[c, :, pl.ds(2 - b, height), pl.ds(2 - a, frames)].reshape(depth, rank)

        early = (y + r + 2) % RING if r in EARLY else SLAB

        def pair(i):
            both = jnp.concatenate([columns(2 * i), columns(2 * i + 1)], axis=1)
            for m in range(3):
                rows = channels // 3
                value = jnp.dot(act_t[m * rows:(m + 1) * rows], both, preferred_element_type=F32)
                for s in range(2):
                    at = pl.multiple_of((2 * i + s) * channels + m * rows, rows)
                    slab[r, pl.ds(at, rows)] = value[:, s * rank:(s + 1) * rank]

        def step(i, _):
            @pl.when(i != early)
            def _():
                pair(i)

            return 0

        if pairs is None:
            pair(early)
        else:
            lax.fori_loop(pairs[0], pairs[1], step, 0)

    for r in EARLY:
        compute(r, None)

    for slot in range(2):
        for copy, h in zip(halo_copies[slot], outer):
            copy.wait_recv()
            extend(slot, h)

    def window(r, e, mine, o):
        owner = (y + r) % RING * 2 + e
        place = mine * RING + o if e == 0 else o * RING + mine
        start = 27 * owner - 27 * (owner - e) // 8 * 8
        at = start * (channels // 8) + OWN * place // 16 * 16
        return slab[r, pl.ds(pl.multiple_of(at, 16), WIN)]

    first_axis = ("x", "z")
    last_axis = ("z", "x")
    first_at = (x, z)
    last_at = (z, x)
    half = RING // 2
    step1, step2, step3, step4, step5 = {}, {}, {}, {}, {}
    turn1, turn2, turn3 = {}, {}, {}

    def add(pieces):
        return functools.reduce(lambda a, b: a + b.astype(F32), pieces)

    def start1(n):
        r, e = CHUNKS[n]
        cut = 1 + n // 2 % 2
        for o in range(1, RING):
            send1[n, o - 1] = window(r, e, (first_at[e] + 2) % RING, o).astype(BF16)
        step1[n] = [
            send(send1.at[n, :cut], recv1.at[n, :cut], along(first_axis[e], 1)),
            send(send1.at[n, cut:], recv1.at[n, cut:], along(first_axis[e], 3)),
        ]

    def start2(n, s):
        r, e = CHUNKS[n]
        cut = 1 + n // 2 % 2
        step = 1 + 2 * s
        step1[n][s].wait_recv()
        for o in range(1, RING):
            value = window(r, e, (first_at[e] + step) % RING, o)
            if (o <= cut) == (s == 0):
                value = add([value, recv1[n, o - 1]])
            send2[n, s, o - 1] = value.astype(BF16)
        step2.setdefault(n, []).append(
            send(send2.at[n, s], recv2.at[n, s], along(first_axis[e], step))
        )

    def finish1(n):
        r, e = CHUNKS[n]
        cut = 1 + e
        for copy in step2[n]:
            copy.wait_recv()
        if r in (1, 3):
            step3[e][0 if r == 1 else 1].wait_recv()
        if r == 0:
            for copy in step4[e]:
                copy.wait_recv()
        for o in range(1, RING):
            p = o - 1
            value = add([window(r, e, first_at[e], o), recv2[n, 0, p], recv2[n, 1, p]])
            if r == 2:
                send3[e, p] = value.astype(STAGE2)
            elif r == 0:
                part2[e, o] = add([value, recv4[e, 0, p], recv4[e, 1, p]])
            else:
                s = 0 if r == 1 else 1
                if (o <= cut) == (s == 0):
                    value = add([value, recv3[e, p]])
                send4[e, s, p] = value.astype(STAGE2)
        if r == 2:
            step3[e] = [
                send(send3.at[e, :cut], recv3.at[e, :cut], along("y", 1)),
                send(send3.at[e, cut:], recv3.at[e, cut:], along("y", 3)),
            ]
        elif r in (1, 3):
            s = 0 if r == 1 else 1
            step4.setdefault(e, []).append(send(send4.at[e, s], recv4.at[e, s], along("y", r)))

    def turn(n):
        r, e = CHUNKS[n]
        s = 0 if r == 1 else 1
        if r in (1, 3):
            turn1[e][s].wait_recv()
        if r == 0:
            for copy in turn2[e]:
                copy.wait_recv()
        for a in range(RING):
            value = window(r, e, a, 0)
            if r == 2:
                send6[e, a] = value.astype(BF16)
            elif r == 0:
                value = add([value, recv8[e, 0, a], recv8[e, 1, a]])
                send9[e, a] = value.astype(STAGE2)
                mine[e, a] = value
            else:
                if (a < half) == (s == 0):
                    value = add([value, recv9[e, a]])
                send8[e, s, a] = value.astype(BF16)
        if r == 2:
            turn1[e] = [
                send(send6.at[e, :half], recv9.at[e, :half], along("y", 1)),
                send(send6.at[e, half:], recv9.at[e, half:], along("y", 3)),
            ]
        elif r == 0:
            turn3[e] = [
                send(send9.at[e, (first_at[e] + j) % RING], recv10.at[e, j - 1], along(first_axis[e], j))
                for j in (2, 1, 3)
            ]
        else:
            turn2.setdefault(e, []).append(send(send8.at[e, s], recv8.at[e, s], along("y", r)))

    def finish2(e):
        for copy in turn3[e]:
            copy.wait_recv()
        part2[e, 0] = add([mine[e, first_at[e]], recv10[e, 0], recv10[e, 1], recv10[e, 2]])
        step5[e] = [
            send(part2.at[e, (last_at[e] + j) % RING], recv5.at[e, j - 1], along(last_axis[e], j))
            for j in (2, 1, 3)
        ]

    for entry in SCHEDULE:
        n = int(entry[1:])
        if entry[0] == "C":
            r, e = CHUNKS[n]
            compute(r, ((0, 3), (3, 4))[e])
        elif entry[0] in "PM":
            start2(n, "PM".index(entry[0]))
        else:
            {"S": start1, "T": turn, "F": finish1, "Z": finish2}[entry[0]](n)

    shift = 2 * space % 16
    row = lax.broadcasted_iota(jnp.int32, (WIN, rank), 0)
    product = jnp.zeros((rank, rank), F32)
    for e in range(2):
        for copy in step5[e]:
            copy.wait_recv()
        value = part2[e, last_at[e]] + recv5[e, 0] + recv5[e, 1] + recv5[e, 2]
        value = pltpu.roll(value, (WIN - shift) % WIN, 0)
        value = jnp.where(row < OWN, value, 0.0)
        rolled[e] = value
        product = product + lax.dot_general(
            value, value, (((0,), (0,)), ((), ())), precision=HIGHEST, preferred_element_type=F32
        )
    gram[...] = product.reshape(spaces, rank // spaces, rank)

    copies = [send(gram.at[to["space"]], recv6.at[n], to) for n, to in enumerate(plane)]
    rows_copy = send(rolled.at[1 - core], rows_in, partner)
    settle(len(sent) - len(copies) - 1)
    value = gram[space]
    for n, copy in reversed(list(enumerate(copies))):
        copy.wait_recv()
        value = value + recv6[n]
    part[0] = value
    copies = [send(part.at[0], recv7.at[n], to) for n, to in enumerate(stack)]
    settle(len(sent) - len(copies))
    for n, copy in enumerate(copies):
        copy.wait_recv()
        value = value + recv7[n]
    part[1] = value
    full[space] = value
    copies = [send(part.at[1], full.at[space], to) for to in plane]
    settle(len(sent) - len(copies))
    for copy in copies:
        copy.wait_recv()

    work[...] = full[...].reshape(rank, rank)
    factor(work, inverse)
    copy = send(inverse, inverse_in, partner)
    settle(len(sent) - 1)

    def solve(rows, lower):
        value = lax.dot_general(
            rows, lower, (((1,), (1,)), ((), ())), precision=HIGHEST, preferred_element_type=F32
        )
        return (value * scale)[:OWN]

    near = solve(rolled[core], inverse[...])
    rows_copy.wait_recv()
    copy.wait_recv()
    far = solve(rows_in[...], inverse_in[...])
    out[:, 0] = jnp.where(core == 0, near, far)
    out[:, 1] = jnp.where(core == 0, far, near)
    settle(len(sent))


def shards(activations, out_grads, omega):
    layers, clips, frames, height, width, channels = activations.shape
    rank = omega.shape[1]
    chunks = len(CHUNKS)
    vmem = pl.BlockSpec(memory_space=pltpu.VMEM)
    blocks, fewer = (RING, WIN, rank), (RING - 1, WIN, rank)
    gram_blocks = (RING * RING, rank // (RING * RING), rank)
    basis = pl.pallas_call(
        functools.partial(reduce_kernel, scale=math.sqrt(27 * channels)),
        name="refresh",
        out_shape=jax.ShapeDtypeStruct((OWN, layers, rank), F32),
        in_specs=[pl.BlockSpec(memory_space=pltpu.HBM)] * 3,
        out_specs=vmem,
        scratch_shapes=[
            pltpu.VMEM(omega.shape, BF16),
            pltpu.VMEM(activations.shape[1:], BF16),
            pltpu.VMEM(activations.shape, BF16),
            pltpu.VMEM(activations.shape[1:], BF16),
            pltpu.VMEM((channels, 2 * height * frames * width), BF16),
            pltpu.VMEM((height, frames, width, rank), BF16),
            pltpu.VMEM((2, height + 2, frames, width, rank), BF16),
            pltpu.VMEM((3, 2, height + 2, frames + 2, width, rank), BF16),
            pltpu.VMEM((RING, SLAB * channels, rank), F32),
            pltpu.VMEM((chunks,) + fewer, BF16),
            pltpu.VMEM((chunks,) + fewer, BF16),
            pltpu.VMEM((chunks, 2) + fewer, BF16),
            pltpu.VMEM((chunks, 2) + fewer, BF16),
            pltpu.VMEM((2,) + fewer, STAGE2),
            pltpu.VMEM((2,) + fewer, STAGE2),
            pltpu.VMEM((2, 2) + fewer, STAGE2),
            pltpu.VMEM((2, 2) + fewer, STAGE2),
            pltpu.VMEM((2,) + blocks, BF16),
            pltpu.VMEM((2,) + blocks, BF16),
            pltpu.VMEM((2, 2) + blocks, BF16),
            pltpu.VMEM((2, 2) + blocks, BF16),
            pltpu.VMEM((2,) + blocks, STAGE2),
            pltpu.VMEM((2,) + fewer, STAGE2),
            pltpu.VMEM((2,) + blocks, F32),
            pltpu.VMEM((2,) + blocks, F32),
            pltpu.VMEM((2, 3, WIN, rank), F32),
            pltpu.VMEM((2, WIN, rank), F32),
            pltpu.VMEM(gram_blocks, F32),
            pltpu.VMEM((RING * RING - 1,) + gram_blocks[1:], F32),
            pltpu.VMEM((2,) + gram_blocks[1:], F32),
            pltpu.VMEM((RING - 1,) + gram_blocks[1:], F32),
            pltpu.VMEM(gram_blocks, F32),
            pltpu.VMEM((WIN, rank), F32),
            pltpu.VMEM((rank, rank), F32),
            pltpu.VMEM((rank, rank), F32),
            pltpu.VMEM((rank, rank), F32),
            pltpu.SemaphoreType.DMA((112,)),
            pltpu.SemaphoreType.DMA((112,)),
            pltpu.SemaphoreType.DMA((4,)),
        ],
        compiler_params=pltpu.CompilerParams(
            collective_id=0, has_side_effects=True, vmem_limit_bytes=13721 * 4096
        ),
    )(activations, out_grads, omega)
    return jnp.transpose(basis, (1, 0, 2))


def solution(mesh):
    return jax.shard_map(
        shards,
        mesh=mesh,
        in_specs=(
            P(None, "dp", None, "space", None, None),
            P(None, "dp", None, "space", None, None),
            P(),
        ),
        out_specs=P(None, ("dp", "space"), None),
        check_vma=False,
    )
```
